512 devices in a mesh: tm: 8 (over y, core), space: 64 (over z, x).
Axes of the slice: x: 4, y: 4, z: 16, core: 2. Of those that a mesh axis runs over, the one named last changes fastest.
Arguments:
- bases: bfloat16 [8, 524288, 128], P('tm', 'space'), may hold values from -12 to 12
- sing_values: float32 [8, 128], P('tm'), may hold values from 0.5 to 4
Outputs:
- merged_bases: bfloat16 [8, 524288, 128], P('tm', 'space')
- merged_values: float32 [8, 128], P('tm')
The draws below stay inside these ranges and needn't reach their ends.
All inputs are finite; a program needn't handle non-finite values.
Results may differ from the reference program's by a relative error of at most 0.0051.
Values may be sent and summed in bfloat16 or wider, within the bound.
No kernel may reach another device: no remote copies, remote signals or barrier semaphores. Data moves between devices by JAX's collectives and lax.ppermute only.
A program may use at most 64 MiB of HBM per device.

```python
import math
import jax
import jax.numpy as jnp
from jax import lax

K = 128
ITERS = 3
NS_STEPS = 6
GROUPS = 8
POINTS = 524288


def draw_bases(key, part):
    key = jax.random.fold_in(key, 11)
    key_latent, key_noise, key_rough, key_perm, key_coef, key_sign, key_region = jax.random.split(key, 7)
    position = jnp.arange(POINTS, dtype=jnp.int32)
    ramp = 1.0 + 2.0 * position.astype(jnp.float32)[None, :, None] / POINTS
    region = position * 8 // POINTS
    rough = jnp.exp(jax.random.uniform(key_rough, (GROUPS, POINTS, 1), jnp.float32, -0.7, 0.7))
    latent = jnp.clip(jax.random.normal(key_latent, (POINTS, K), jnp.float32), -4.0, 4.0)
    noise = 0.6 * jnp.clip(jax.random.normal(key_noise, (GROUPS, POINTS, K), jnp.float32), -4.0, 4.0)
    perm_keys = jax.random.split(key_perm, GROUPS * 4)
    perms = jax.vmap(lambda single: jax.random.permutation(single, K))(perm_keys).astype(jnp.int32)
    perms = perms.reshape(GROUPS, 4, K)
    magnitude = jax.random.uniform(key_coef, (GROUPS, 3, 1, K), jnp.float32, 0.25, 0.5)
    signs = jnp.where(jax.random.bernoulli(key_sign, 0.5, (GROUPS, 3, 1, K)), 1.0, -1.0)
    factor = 1.0 + jax.random.uniform(key_region, (GROUPS, 3, 8, K), jnp.float32, -0.6, 0.6)
    coef = magnitude * signs * factor
    mixed = jnp.transpose(jnp.take(latent, perms[:, 0], axis=1), (1, 0, 2))
    for term in range(1, 4):
        weights = jnp.take(coef[:, term - 1], region, axis=1)
        shifted = jnp.transpose(jnp.take(latent, perms[:, term], axis=1), (1, 0, 2))
        mixed = mixed + weights * shifted
    values = (mixed + noise) * ramp * rough / 3.3
    return jnp.clip(values, -12.0, 12.0).astype(jnp.bfloat16)


def block_levels(stream_key, extent, pieces, least, largest):
    gain, own = 1.0, jax.random.fold_in(stream_key, 6)
    for dim, shards_of in pieces:
        draws = jnp.exp(jax.random.uniform(jax.random.fold_in(own, dim), (shards_of,), jnp.float32, least / len(pieces), largest / len(pieces)))
        gain = gain * jnp.repeat(draws, extent[dim] // shards_of).reshape([-1 if axis == dim else 1 for axis in range(len(extent))])
    return gain


def setup_inputs(seed: int = 0) -> dict:
    splits = jax.random.split(jax.random.key(seed), 3)
    return {
        "bases": draw_bases(jax.random.fold_in(splits[2], 71), 0),
        "sing_values": jnp.clip(jnp.exp(math.log(4.0) - 2.0794415 * jax.random.uniform(splits[1], (GROUPS, K), jnp.float32) ** block_levels(splits[1], (GROUPS, K), ((0, 8),), -0.2, 0.2)), 0.5, 4.0),
    }


def polar_iterate(gram):
    eye = jnp.eye(K, dtype=jnp.float32)
    start = jnp.concatenate([eye, eye], axis=0) / jnp.sqrt(jnp.float32(2.0))
    for outer in range(ITERS):
        y = jnp.dot(gram, start, precision=lax.Precision.HIGHEST)
        y = y / jnp.sqrt(jnp.sum(y * y) + 1e-06)
        for inner in range(NS_STEPS):
            inner_prod = jnp.dot(y.T, y, precision=lax.Precision.HIGHEST)
            y = 1.5 * y - 0.5 * jnp.dot(y, inner_prod, precision=lax.Precision.HIGHEST)
        start = y
    return start

def reference(bases, sing_values):
    weighted = (bases.astype(jnp.float32) * sing_values[:, None, :]).astype(jnp.bfloat16)
    outs_b = []
    outs_v = []
    for group in range(GROUPS):
        partner = group ^ 1
        stacked = jnp.concatenate([weighted[group], weighted[partner]], axis=1)
        gram = jnp.dot(stacked.T, stacked, preferred_element_type=jnp.float32)
        rotation = polar_iterate(gram).astype(jnp.bfloat16)
        merged = jnp.dot(stacked, rotation, preferred_element_type=jnp.float32)
        values = jnp.sqrt(lax.optimization_barrier(jnp.sum(merged * merged, axis=0)) / POINTS + 1e-06)
        outs_b.append((merged / values[None, :]).astype(jnp.bfloat16))
        outs_v.append(values)
    return (jnp.stack(outs_b), jnp.stack(outs_v))
```

```python
import jax
import jax.numpy as jnp
from jax import lax
from jax.experimental import pallas as pl
from jax.experimental.pallas import tpu as pltpu
from jax.sharding import Mesh, PartitionSpec as P

ITERS = 3
NS_STEPS = 6
GRAM_BLOCK = 1024


def gram_kernel(core_ref, own_ref, other_ref, out_ref, acc_ref):
    step = pl.program_id(0)
    stacked = jnp.concatenate([own_ref[...], other_ref[...]], axis=1)
    part = lax.dot_general(
        stacked, stacked, (((0,), (0,)), ((), ())), preferred_element_type=jnp.float32
    )

    @pl.when(step == 0)
    def _():
        acc_ref[...] = part

    @pl.when(step > 0)
    def _():
        acc_ref[...] += part

    last = step == pl.num_programs(0) - 1
    w = own_ref.shape[1]

    @pl.when(last & (core_ref[0] == 0))
    def _():
        out_ref[0:w] = acc_ref[:w, :w]
        out_ref[w : 2 * w] = acc_ref[:w, w:]
        out_ref[2 * w :] = acc_ref[w:, w:]

    @pl.when(last & (core_ref[0] == 1))
    def _():
        out_ref[0:w] = acc_ref[w:, w:]
        out_ref[w : 2 * w] = acc_ref[w:, :w]
        out_ref[2 * w :] = acc_ref[:w, :w]


def half_gram(own, other, core):
    rows, w = own.shape
    steps = rows // 2 // GRAM_BLOCK
    spec = pl.BlockSpec((GRAM_BLOCK, w), lambda i, core_ref: (core_ref[0] * steps + i, 0))
    return pl.pallas_call(
        gram_kernel,
        grid_spec=pltpu.PrefetchScalarGridSpec(
            num_scalar_prefetch=1,
            grid=(steps,),
            in_specs=[spec, spec],
            out_specs=pl.BlockSpec((3 * w, w), lambda i, core_ref: (0, 0)),
            scratch_shapes=[pltpu.VMEM((2 * w, 2 * w), jnp.float32)],
        ),
        out_shape=jax.ShapeDtypeStruct((3 * w, w), jnp.float32),
        compiler_params=pltpu.CompilerParams(vmem_limit_bytes=16 << 20),
    )(core, own, other)


def sum_over_chips(part):
    rows, w = part.shape
    near = ("core", "x")
    n = lax.axis_size("core") * lax.axis_size("x")
    part = lax.all_to_all(part.reshape(n, rows // n, w), near, 0, 0)
    part = jnp.sum(part, axis=0).astype(jnp.bfloat16)
    far = lax.axis_size("z")
    part = lax.all_to_all(jnp.broadcast_to(part[None], (far, rows // n, w)), "z", 0, 0)
    part = jnp.sum(part.astype(jnp.float32), axis=0)
    part = lax.all_to_all(jnp.broadcast_to(part[None], (n, rows // n, w)), near, 0, 0)
    return part.reshape(rows, w)


def polar_iterate(gram, width):
    eye = jnp.eye(width, dtype=jnp.float32)
    start = jnp.concatenate([eye, eye], axis=0) / jnp.sqrt(jnp.float32(2.0))
    for outer in range(ITERS):
        y = jnp.dot(gram, start, precision=lax.Precision.HIGHEST)
        y = y / jnp.sqrt(jnp.sum(y * y) + 1e-06)
        for inner in range(NS_STEPS):
            inner_prod = jnp.dot(y.T, y, precision=lax.Precision.HIGHEST)
            y = 1.5 * y - 0.5 * jnp.dot(y, inner_prod, precision=lax.Precision.HIGHEST)
        start = y
    return start


def local(bases, sing_values):
    width = bases.shape[2]
    rows = bases.shape[1]
    points_all = rows * lax.axis_size("z") * lax.axis_size("x")
    core = lax.axis_index("core")
    own = (bases[0].astype(jnp.float32) * sing_values[0][None, :]).astype(jnp.bfloat16)
    other = lax.ppermute(own, "core", [(0, 1), (1, 0)])
    blocks = sum_over_chips(half_gram(own, other, core.astype(jnp.int32)[None]))
    aa, ab, bb = blocks[:width], blocks[width : 2 * width], blocks[2 * width :]
    gram = jnp.concatenate(
        [jnp.concatenate([aa, ab], axis=1), jnp.concatenate([ab.T, bb], axis=1)], axis=0
    )
    rotation = polar_iterate(gram, width).astype(jnp.bfloat16)
    wide = rotation.astype(jnp.float32)
    squares = jnp.sum(wide * jnp.dot(gram, wide, precision=lax.Precision.HIGHEST), axis=0)
    values = jnp.sqrt(jnp.maximum(squares, 0.0) / points_all + 1e-06)
    first, second = rotation[:width], rotation[width:]
    mine = jnp.where(core == 0, first, second)
    theirs = jnp.where(core == 0, second, first)
    merged = jnp.dot(own, mine, preferred_element_type=jnp.float32)
    merged = merged + jnp.dot(other, theirs, preferred_element_type=jnp.float32)
    merged_bases = (merged / values[None, :]).astype(jnp.bfloat16)
    return (merged_bases[None], values[None])


def solution(mesh):
    fine = Mesh(mesh.devices.reshape(-1, 2, 16, 4), ("y", "core", "z", "x"))
    specs = (P(("y", "core"), ("z", "x"), None), P(("y", "core"), None))
    return jax.shard_map(local, mesh=fine, in_specs=specs, out_specs=specs, check_vma=False)
```

```python
import functools
import math

import jax
import jax.numpy as jnp
from jax import lax
from jax.experimental import pallas as pl
from jax.experimental.pallas import tpu as pltpu
from jax.sharding import Mesh, PartitionSpec as P

ITERS = 3
NS_STEPS = 6
CHUNK = 1024
ROWS = (((0,), (0,)), ((), ()))
PLAIN = (((1,), (0,)), ((), ()))
COLUMNS = (((1,), (1,)), ((), ()))
bf16 = jnp.bfloat16
f32 = jnp.float32


def dot(a, b, dims=PLAIN):
    return lax.dot_general(a, b, dims, preferred_element_type=f32)


def split(x):
    high = x.astype(bf16)
    return high, (x - high.astype(f32)).astype(bf16)


def wide_dot(a, b, dims=PLAIN):
    axis = 1 if dims is PLAIN else 0
    n = b.shape[axis]
    right = jnp.concatenate(split(b), axis=axis)
    right = jnp.concatenate([right, right], axis=1 - axis)
    both = dot(jnp.concatenate(split(a), axis=1), right, dims)
    return both[:, :n] + both[:, n:]


def polar_iterate(gram):
    w = gram.shape[0] // 2
    diag = lax.broadcasted_iota(jnp.int32, (w, w), 0) == lax.broadcasted_iota(jnp.int32, (w, w), 1)
    yt = (gram[:w] + gram[w:]) * f32(1.0 / math.sqrt(2.0))
    for outer in range(ITERS):
        if outer:
            yt = wide_dot(start, gram)
        scale = 1.0 / (jnp.sum(yt * yt) + 1e-06)
        m = wide_dot(yt, yt, COLUMNS) * scale
        yt = yt * jnp.sqrt(scale)
        square = wide_dot(m, m)
        q = 1.5 * diag.astype(f32) - 0.5 * m
        for inner in range(1, NS_STEPS):
            m = 2.25 * m - 1.5 * square + 0.25 * wide_dot(square, m)
            if inner < NS_STEPS - 1:
                both = wide_dot(jnp.concatenate([m, q], axis=0), m)
                square = both[:w]
                q = 1.5 * q - 0.5 * both[w:]
        u = wide_dot(q, yt)
        start = 1.5 * u - 0.5 * wide_dot(m, u)
    return start


def column_squares(gram, rotation):
    high, rest = split(gram)
    low = (gram - high.astype(f32) - rest.astype(f32)).astype(bf16)
    turned = dot(rotation, high) + (dot(rotation, rest) + dot(rotation, low))
    return jnp.sum((turned * rotation.astype(f32)).T, axis=0, keepdims=True)


def finish_kernel(
    points, core_ref, gram_ref, own_a, own_b, other_a, other_b, out_ref, values_ref, rows_ref, sem
):
    w = gram_ref.shape[1]
    aa, ab, bb = gram_ref[:w], gram_ref[w : 2 * w], gram_ref[2 * w :]
    gram = jnp.concatenate(
        [jnp.concatenate([aa, ab], axis=1), jnp.concatenate([ab.T, bb], axis=1)], axis=0
    )
    rotation = polar_iterate(gram).astype(bf16)
    squares = column_squares(gram, rotation)
    values = jnp.sqrt(jnp.maximum(squares, 0.0) / points + 1e-06)
    values_ref[...] = values
    inverse = 1.0 / values
    core = core_ref[0]
    swapped = jnp.concatenate([rotation[:, w:], rotation[:, :w]], axis=1)
    rotation = jnp.where(core == 0, rotation, swapped)
    half = own_a.shape[0]
    copies = []
    for part, (own, other, first) in enumerate(
        [(own_a, other_a, core * half), (own_b, other_b, (1 - core) * half)]
    ):
        for j in range(half // CHUNK):
            rows = pl.ds(j * CHUNK, CHUNK)
            stacked = jnp.concatenate([own[rows], other[rows]], axis=1)
            k = part * (half // CHUNK) + j
            here = rows_ref.at[pl.ds(k * CHUNK, CHUNK)]
            here[...] = (dot(stacked, rotation, COLUMNS) * inverse).astype(bf16)
            there = out_ref.at[pl.ds(pl.multiple_of(first + j * CHUNK, CHUNK), CHUNK)]
            copies.append(pltpu.make_async_copy(here, there, sem.at[k]))
            copies[-1].start()
    for copy in copies:
        copy.wait()


def finish(core, blocks, own_a, own_b, other_a, other_b, points):
    half, w = own_a.shape
    vmem = pl.BlockSpec(memory_space=pltpu.VMEM)
    return pl.pallas_call(
        functools.partial(finish_kernel, points),
        in_specs=[pl.BlockSpec(memory_space=pltpu.SMEM)] + [vmem] * 5,
        out_specs=[pl.BlockSpec(memory_space=pl.ANY), vmem],
        out_shape=[jax.ShapeDtypeStruct((2 * half, w), bf16), jax.ShapeDtypeStruct((1, w), f32)],
        scratch_shapes=[
            pltpu.VMEM((2 * half, w), bf16),
            pltpu.SemaphoreType.DMA((2 * half // CHUNK,)),
        ],
        compiler_params=pltpu.CompilerParams(vmem_limit_bytes=24 << 20),
    )(core, blocks, own_a, own_b, other_a, other_b)


def gram_kernel(core_ref, own_ref, other_ref, out_ref):
    w = own_ref.shape[1]
    stacked = jnp.concatenate([own_ref[...], other_ref[...]], axis=1)
    gram = dot(stacked, stacked, ROWS)

    @pl.when(core_ref[0] == 0)
    def _():
        out_ref[0:w] = gram[:w, :w]
        out_ref[w : 2 * w] = gram[:w, w:]
        out_ref[2 * w :] = gram[w:, w:]

    @pl.when(core_ref[0] != 0)
    def _():
        out_ref[0:w] = gram[w:, w:]
        out_ref[w : 2 * w] = gram[w:, :w]
        out_ref[2 * w :] = gram[:w, :w]


def half_gram(core, own, other):
    w = own.shape[1]
    vmem = pl.BlockSpec(memory_space=pltpu.VMEM)
    return pl.pallas_call(
        gram_kernel,
        in_specs=[pl.BlockSpec(memory_space=pltpu.SMEM), vmem, vmem],
        out_specs=vmem,
        out_shape=jax.ShapeDtypeStruct((3 * w, w), f32),
        compiler_params=pltpu.CompilerParams(vmem_limit_bytes=24 << 20),
    )(core, own, other)


def sum_over_chips(part):
    rows, w = part.shape
    near = ("core", "x")
    n = lax.axis_size("core") * lax.axis_size("x")
    part = lax.all_to_all(part.reshape(n, rows // n, w), near, 0, 0)
    part = jnp.sum(part, axis=0).astype(bf16)
    far = lax.axis_size("z")
    part = lax.all_to_all(jnp.broadcast_to(part[None], (far, rows // n, w)), "z", 0, 0)
    part = jnp.sum(part.astype(f32), axis=0)
    part = lax.all_to_all(jnp.broadcast_to(part[None], (n, rows // n, w)), near, 0, 0)
    return part.reshape(rows, w)


def local(bases, sing_values):
    rows = bases.shape[1]
    half = rows // 2
    points = rows * lax.axis_size("z") * lax.axis_size("x")
    core = lax.axis_index("core").astype(jnp.int32)

    def weighted(first):
        part = lax.dynamic_slice_in_dim(bases[0], first, half)
        return (part.astype(f32) * sing_values[0][None, :]).astype(bf16)

    def partners(value):
        return lax.ppermute(value, "core", [(0, 1), (1, 0)])

    own_b = weighted((1 - core) * half)
    other_a = partners(own_b)
    own_a = weighted(core * half)
    other_b = partners(own_a)
    blocks = sum_over_chips(half_gram(core[None], own_a, other_a))
    merged, values = finish(core[None], blocks, own_a, own_b, other_a, other_b, points)
    return (merged[None], values)


def solution(mesh):
    fine = Mesh(mesh.devices.reshape(-1, 2, 16, 4), ("y", "core", "z", "x"))
    specs = (P(("y", "core"), ("z", "x"), None), P(("y", "core"), None))
    return jax.shard_map(local, mesh=fine, in_specs=specs, out_specs=specs, check_vma=False)
```

```python
import functools
import math

import jax
import jax.numpy as jnp
from jax import lax
from jax.experimental import pallas as pl
from jax.experimental.pallas import tpu as pltpu
from jax.sharding import Mesh, PartitionSpec as P

ITERS = 3
NS_STEPS = 6
CHUNK = 1024
ROWS = (((0,), (0,)), ((), ()))
PLAIN = (((1,), (0,)), ((), ()))
COLUMNS = (((1,), (1,)), ((), ()))
bf16 = jnp.bfloat16
f32 = jnp.float32


def dot(a, b, dims=PLAIN):
    return lax.dot_general(a, b, dims, preferred_element_type=f32)


def split(x):
    high = x.astype(bf16)
    return high, (x - high.astype(f32)).astype(bf16)


def wide_dot(a, b, dims=PLAIN):
    axis = 1 if dims is PLAIN else 0
    n = b.shape[axis]
    right = jnp.concatenate(split(b), axis=axis)
    right = jnp.concatenate([right, right], axis=1 - axis)
    both = dot(jnp.concatenate(split(a), axis=1), right, dims)
    return both[:, :n] + both[:, n:]


def polar_iterate(gram):
    w = gram.shape[0] // 2
    diag = lax.broadcasted_iota(jnp.int32, (w, w), 0) == lax.broadcasted_iota(jnp.int32, (w, w), 1)
    yt = (gram[:w] + gram[w:]) * f32(1.0 / math.sqrt(2.0))
    for outer in range(ITERS):
        if outer:
            yt = wide_dot(start, gram)
        scale = 1.0 / (jnp.sum(yt * yt) + 1e-06)
        m = wide_dot(yt, yt, COLUMNS) * scale
        yt = yt * jnp.sqrt(scale)
        square = wide_dot(m, m)
        q = 1.5 * diag.astype(f32) - 0.5 * m
        for inner in range(1, NS_STEPS):
            m = 2.25 * m - 1.5 * square + 0.25 * wide_dot(square, m)
            if inner < NS_STEPS - 1:
                both = wide_dot(jnp.concatenate([m, q], axis=0), m)
                square = both[:w]
                q = 1.5 * q - 0.5 * both[w:]
        u = wide_dot(q, yt)
        start = 1.5 * u - 0.5 * wide_dot(m, u)
    return start


def column_squares(gram, rotation):
    high, rest = split(gram)
    low = (gram - high.astype(f32) - rest.astype(f32)).astype(bf16)
    turned = dot(rotation, high) + (dot(rotation, rest) + dot(rotation, low))
    return jnp.sum((turned * rotation.astype(f32)).T, axis=0, keepdims=True)


def finish_kernel(
    points, core_ref, gram_ref, weights_hbm, bases_ref, near_ref, far_ref,
    out_ref, values_ref, weights_ref, own_ref, other_ref, rows_ref, sem, out_sem,
):
    core = core_ref[0]
    rows, w = own_ref.shape
    half = rows // 2
    here, there = (pl.ds(pl.multiple_of(c * half, half), half) for c in (core, 1 - core))
    loads = [
        pltpu.make_async_copy(bases_ref, own_ref, sem.at[0]),
        pltpu.make_async_copy(near_ref, other_ref.at[here], sem.at[1]),
        pltpu.make_async_copy(far_ref, other_ref.at[there], sem.at[2]),
        pltpu.make_async_copy(weights_hbm, weights_ref, sem.at[3]),
    ]
    for load in loads:
        load.start()
    aa, ab, bb = gram_ref[:w], gram_ref[w : 2 * w], gram_ref[2 * w :]
    gram = jnp.concatenate(
        [jnp.concatenate([aa, ab], axis=1), jnp.concatenate([ab.T, bb], axis=1)], axis=0
    )
    rotation = polar_iterate(gram).astype(bf16)
    squares = column_squares(gram, rotation)
    values = jnp.sqrt(jnp.maximum(squares, 0.0) / points + 1e-06)
    values_ref[...] = values
    inverse = 1.0 / values
    swapped = jnp.concatenate([rotation[:, w:], rotation[:, :w]], axis=1)
    rotation = jnp.where(core == 0, rotation, swapped)
    for load in loads:
        load.wait()
    copies = []
    for j in range(rows // CHUNK):
        part = pl.ds(j * CHUNK, CHUNK)
        own = (own_ref[part].astype(f32) * weights_ref[...]).astype(bf16)
        stacked = jnp.concatenate([own, other_ref[part]], axis=1)
        rows_ref[part] = (dot(stacked, rotation, COLUMNS) * inverse).astype(bf16)
        copies.append(pltpu.make_async_copy(rows_ref.at[part], out_ref.at[part], out_sem.at[j]))
        copies[-1].start()
    for copy in copies:
        copy.wait()


def finish(core, blocks, sing_values, bases, near, far, points):
    rows, w = bases.shape
    vmem = pl.BlockSpec(memory_space=pltpu.VMEM)
    anywhere = pl.BlockSpec(memory_space=pl.ANY)
    return pl.pallas_call(
        functools.partial(finish_kernel, points),
        in_specs=[pl.BlockSpec(memory_space=pltpu.SMEM), vmem]
        + [pl.BlockSpec(memory_space=pltpu.HBM)] * 2
        + [anywhere] * 2,
        out_specs=[anywhere, vmem],
        out_shape=[jax.ShapeDtypeStruct((rows, w), bf16), jax.ShapeDtypeStruct((1, w), f32)],
        scratch_shapes=[
            pltpu.VMEM(sing_values.shape, f32),
            pltpu.VMEM((rows, w), bf16),
            pltpu.VMEM((rows, w), bf16),
            pltpu.VMEM((rows, w), bf16),
            pltpu.SemaphoreType.DMA((4,)),
            pltpu.SemaphoreType.DMA((rows // CHUNK,)),
        ],
        compiler_params=pltpu.CompilerParams(vmem_limit_bytes=16 << 20),
    )(core, blocks, sing_values, bases, near, far)


def weigh_kernel(block_ref, weights_hbm, bases_ref, out_ref, weights_ref, rows_ref, sem):
    half = out_ref.shape[0]
    weights = pltpu.make_async_copy(weights_hbm, weights_ref, sem.at[half // CHUNK])
    weights.start()
    copies = []
    for j in range(half // CHUNK):
        first = pl.multiple_of(block_ref[0] * half + j * CHUNK, CHUNK)
        here = rows_ref.at[pl.ds(j * CHUNK, CHUNK)]
        copies.append(pltpu.make_async_copy(bases_ref.at[pl.ds(first, CHUNK)], here, sem.at[j]))
        copies[-1].start()
    weights.wait()
    for j, copy in enumerate(copies):
        copy.wait()
        rows = pl.ds(j * CHUNK, CHUNK)
        out_ref[rows] = (rows_ref[rows].astype(f32) * weights_ref[...]).astype(bf16)


def weigh_half(block, sing_values, bases):
    rows, w = bases.shape
    half = rows // 2
    vmem = pl.BlockSpec(memory_space=pltpu.VMEM)
    return pl.pallas_call(
        weigh_kernel,
        in_specs=[pl.BlockSpec(memory_space=pltpu.SMEM)] + [pl.BlockSpec(memory_space=pltpu.HBM)] * 2,
        out_specs=vmem,
        out_shape=pltpu.VMEM((half, w), bf16),
        scratch_shapes=[
            pltpu.VMEM(sing_values.shape, f32),
            pltpu.VMEM((half, w), bf16),
            pltpu.SemaphoreType.DMA((half // CHUNK + 1,)),
        ],
        compiler_params=pltpu.CompilerParams(vmem_limit_bytes=4 << 20),
        cost_estimate=pl.CostEstimate(flops=half * w, bytes_accessed=4 * half * w, transcendentals=0),
    )(block, sing_values, bases)


def gram_kernel(core_ref, own_ref, other_ref, out_ref):
    w = own_ref.shape[1]
    stacked = jnp.concatenate([own_ref[...], other_ref[...]], axis=1)
    gram = dot(stacked, stacked, ROWS)

    @pl.when(core_ref[0] == 0)
    def _():
        out_ref[0:w] = gram[:w, :w]
        out_ref[w : 2 * w] = gram[:w, w:]
        out_ref[2 * w :] = gram[w:, w:]

    @pl.when(core_ref[0] != 0)
    def _():
        out_ref[0:w] = gram[w:, w:]
        out_ref[w : 2 * w] = gram[w:, :w]
        out_ref[2 * w :] = gram[:w, :w]


def half_gram(core, own, other):
    w = own.shape[1]
    vmem = pl.BlockSpec(memory_space=pltpu.VMEM)
    return pl.pallas_call(
        gram_kernel,
        in_specs=[pl.BlockSpec(memory_space=pltpu.SMEM), vmem, vmem],
        out_specs=vmem,
        out_shape=jax.ShapeDtypeStruct((3 * w, w), f32),
        compiler_params=pltpu.CompilerParams(vmem_limit_bytes=12 << 20),
    )(core, own, other)


def add_kernel(after_ref, parts_ref, out_ref):
    total = jnp.sum(parts_ref[...], axis=0)
    for k in range(out_ref.shape[0]):
        out_ref[k] = total


def add_and_repeat(parts, repeats, after):
    vmem = pl.BlockSpec(memory_space=pltpu.VMEM)
    return pl.pallas_call(
        add_kernel,
        in_specs=[pl.BlockSpec(memory_space=pl.ANY), vmem],
        out_specs=vmem,
        out_shape=jax.ShapeDtypeStruct((repeats, *parts.shape[1:]), f32),
        compiler_params=pltpu.CompilerParams(vmem_limit_bytes=2 << 20),
    )(after, parts)


def sum_over_chips(part, after):
    rows, w = part.shape
    near, far = ("core", "z_lo", "x"), "z_hi"
    n, m = math.prod(lax.axis_size(axis) for axis in near), lax.axis_size(far)
    part = lax.all_to_all(part.reshape(n, rows // n, w), near, 0, 0)
    part = add_and_repeat(part, m, after)
    turned = [[(i + m // 2) % m for i in range(m)]]
    part = lax.all_to_all(part, far, 0, 0, axis_index_groups=turned)
    part = jnp.sum(part, axis=0)
    part = lax.all_to_all(jnp.broadcast_to(part[None], (n, rows // n, w)), near, 0, 0)
    return part.reshape(rows, w)


def local(bases, sing_values):
    rows = bases.shape[1]
    half = rows // 2
    points = rows * math.prod(lax.axis_size(axis) for axis in ("z_hi", "z_lo", "x"))
    core = lax.axis_index("core").astype(jnp.int32)

    def partners(value):
        return lax.ppermute(value, "core", [(0, 1), (1, 0)])

    bases = pltpu.with_memory_space_constraint(bases[0], pltpu.HBM)
    sing_values = pltpu.with_memory_space_constraint(sing_values, pltpu.HBM)
    own_b = weigh_half(1 - core[None], sing_values, bases)
    other_a = partners(own_b)
    own_a = weigh_half(core[None], sing_values, bases)
    other_b = partners(own_a)
    blocks = sum_over_chips(half_gram(core[None], own_a, other_a), other_b)
    merged, values = finish(
        core[None], blocks, sing_values, bases, other_a, other_b, points
    )
    return (merged[None], values)


def solution(mesh):
    fine = Mesh(mesh.devices.reshape(-1, 2, 8, 2, 4), ("y", "core", "z_hi", "z_lo", "x"))
    specs = (P(("y", "core"), ("z_hi", "z_lo", "x"), None), P(("y", "core"), None))
    return jax.shard_map(local, mesh=fine, in_specs=specs, out_specs=specs, check_vma=False)
```

```python
import functools
import math

import jax
import jax.numpy as jnp
from jax import lax
from jax.experimental import pallas as pl
from jax.experimental.pallas import tpu as pltpu
from jax.sharding import Mesh, PartitionSpec as P

ITERS = 3
NS_STEPS = 6
CHUNK = 1024
ROWS = (((0,), (0,)), ((), ()))
PLAIN = (((1,), (0,)), ((), ()))
COLUMNS = (((1,), (1,)), ((), ()))
bf16 = jnp.bfloat16
f32 = jnp.float32


def dot(a, b, dims=PLAIN):
    return lax.dot_general(a, b, dims, preferred_element_type=f32)


def split(x):
    high = x.astype(bf16)
    return high, (x - high.astype(f32)).astype(bf16)


def wide_dot(a, b, dims=PLAIN):
    (a_high, a_low), (b_high, b_low) = split(a), split(b)
    left = jnp.concatenate([a_high, a_low, a_high], axis=1)
    right = jnp.concatenate([b_high, b_high, b_low], axis=0 if dims is PLAIN else 1)
    return dot(left, right, dims)


def polar_iterate(gram):
    w = gram.shape[0] // 2
    diag = lax.broadcasted_iota(jnp.int32, (w, w), 0) == lax.broadcasted_iota(jnp.int32, (w, w), 1)
    yt = (gram[:w] + gram[w:]) * f32(1.0 / math.sqrt(2.0))
    for outer in range(ITERS):
        scale = 1.0 / (jnp.sum(yt * yt) + 1e-06)
        m = wide_dot(yt, yt, COLUMNS) * scale
        yt = yt * jnp.sqrt(scale)
        ahead = yt if outer == ITERS - 1 else wide_dot(yt, gram)
        square = wide_dot(m, m)
        q = 1.5 * diag.astype(f32) - 0.5 * m
        for inner in range(1, NS_STEPS):
            m = 2.25 * m - 1.5 * square + 0.25 * wide_dot(square, m)
            if inner < NS_STEPS - 1:
                both = wide_dot(jnp.concatenate([m, q], axis=0), m)
                square = both[:w]
                q = 1.5 * q - 0.5 * both[w:]
        u = wide_dot(q, ahead)
        yt = 1.5 * u - 0.5 * wide_dot(m, u)
    return yt


def column_squares(gram, rotation):
    high, rest = split(gram)
    low = (gram - high.astype(f32) - rest.astype(f32)).astype(bf16)
    turned = dot(rotation, high) + (dot(rotation, rest) + dot(rotation, low))
    return jnp.sum((turned * rotation.astype(f32)).T, axis=0, keepdims=True)


def finish_kernel(
    points, core_ref, gram_ref, weights_hbm, bases_ref, near_ref, far_ref,
    out_ref, values_ref, gram_rows_ref, weights_ref, own_ref, other_ref, rows_ref, sem, out_sem,
):
    core = core_ref[0]
    rows, w = own_ref.shape
    half = rows // 2
    here, there = (pl.ds(pl.multiple_of(c * half, half), half) for c in (core, 1 - core))
    loads = [
        pltpu.make_async_copy(bases_ref, own_ref, sem.at[0]),
        pltpu.make_async_copy(near_ref, other_ref.at[here], sem.at[1]),
        pltpu.make_async_copy(far_ref, other_ref.at[there], sem.at[2]),
        pltpu.make_async_copy(weights_hbm, weights_ref, sem.at[3]),
    ]
    for load in loads:
        load.start()
    slices, pairs = gram_ref.shape[:2]
    each = w // slices
    for k in range(slices):
        for p in range(pairs - 1):
            first = k * each + 2 * p if 2 * p < each else w + k * each + 2 * p - each
            gram_rows_ref[first : first + 2] = gram_ref[k, p]
    shared, ab = gram_rows_ref[:w], gram_rows_ref[w:]
    turned = shared.T
    row = lax.broadcasted_iota(jnp.int32, (w, w), 0)
    column = lax.broadcasted_iota(jnp.int32, (w, w), 1)
    aa = jnp.where(row <= column, shared, turned)
    bb = jnp.where(row > column, shared, jnp.where(row < column, turned, gram_ref[0, pairs - 1, :1]))
    gram = jnp.concatenate(
        [jnp.concatenate([aa, ab], axis=1), jnp.concatenate([ab.T, bb], axis=1)], axis=0
    )
    rotation = polar_iterate(gram).astype(bf16)
    squares = column_squares(gram, rotation)
    values = jnp.sqrt(jnp.maximum(squares, 0.0) / points + 1e-06)
    values_ref[...] = values
    inverse = 1.0 / values
    swapped = jnp.concatenate([rotation[:, w:], rotation[:, :w]], axis=1)
    rotation = jnp.where(core == 0, rotation, swapped)
    for load in loads:
        load.wait()
    copies = []
    for j in range(rows // CHUNK):
        part = pl.ds(j * CHUNK, CHUNK)
        own = (own_ref[part].astype(f32) * weights_ref[...]).astype(bf16)
        stacked = jnp.concatenate([own, other_ref[part]], axis=1)
        rows_ref[part] = (dot(stacked, rotation, COLUMNS) * inverse).astype(bf16)
        copies.append(pltpu.make_async_copy(rows_ref.at[part], out_ref.at[part], out_sem.at[j]))
        copies[-1].start()
    for copy in copies:
        copy.wait()


def finish(core, blocks, sing_values, bases, near, far, points):
    rows, w = bases.shape
    vmem = pl.BlockSpec(memory_space=pltpu.VMEM)
    anywhere = pl.BlockSpec(memory_space=pl.ANY)
    return pl.pallas_call(
        functools.partial(finish_kernel, points),
        in_specs=[pl.BlockSpec(memory_space=pltpu.SMEM), vmem]
        + [pl.BlockSpec(memory_space=pltpu.HBM)] * 2
        + [anywhere] * 2,
        out_specs=[anywhere, vmem],
        out_shape=[jax.ShapeDtypeStruct((rows, w), bf16), jax.ShapeDtypeStruct((1, w), f32)],
        scratch_shapes=[
            pltpu.VMEM((2 * w, w), f32),
            pltpu.VMEM(sing_values.shape, f32),
            pltpu.VMEM((rows, w), bf16),
            pltpu.VMEM((rows, w), bf16),
            pltpu.VMEM((rows, w), bf16),
            pltpu.SemaphoreType.DMA((4,)),
            pltpu.SemaphoreType.DMA((rows // CHUNK,)),
        ],
        compiler_params=pltpu.CompilerParams(vmem_limit_bytes=16 << 20),
    )(core, blocks, sing_values, bases, near, far)


def weigh_kernel(
    core_ref, weights_hbm, bases_ref, theirs_ref, mine_ref, weights_ref, rows_ref, sem
):
    rows = bases_ref.shape[0]
    steps = rows // 2 // CHUNK
    weights = pltpu.make_async_copy(weights_hbm, weights_ref, sem.at[2 * steps])
    weights.start()
    copies = []
    for part, block in enumerate((1 - core_ref[0], core_ref[0])):
        for j in range(steps):
            first = pl.multiple_of((block * steps + j) * CHUNK, CHUNK)
            here = rows_ref.at[pl.ds((part * steps + j) * CHUNK, CHUNK)]
            there = bases_ref.at[pl.ds(first, CHUNK)]
            copies.append(pltpu.make_async_copy(there, here, sem.at[part * steps + j]))
            copies[-1].start()
    weights.wait()
    for part, out_ref in enumerate((theirs_ref, mine_ref)):
        for j in range(steps):
            copies[part * steps + j].wait()
            taken = rows_ref[pl.ds((part * steps + j) * CHUNK, CHUNK)]
            out_ref[pl.ds(j * CHUNK, CHUNK)] = (taken.astype(f32) * weights_ref[...]).astype(bf16)


def weigh(core, sing_values, bases):
    rows, w = bases.shape
    vmem = pl.BlockSpec(memory_space=pltpu.VMEM)
    return pl.pallas_call(
        weigh_kernel,
        in_specs=[pl.BlockSpec(memory_space=pltpu.SMEM)] + [pl.BlockSpec(memory_space=pltpu.HBM)] * 2,
        out_specs=[vmem] * 2,
        out_shape=[pltpu.VMEM((rows // 2, w), bf16)] * 2,
        scratch_shapes=[
            pltpu.VMEM(sing_values.shape, f32),
            pltpu.VMEM((rows, w), bf16),
            pltpu.SemaphoreType.DMA((rows // CHUNK + 1,)),
        ],
        compiler_params=pltpu.CompilerParams(vmem_limit_bytes=8 << 20),
    )(core, sing_values, bases)


def gram_kernel(own_ref, other_ref, out_ref):
    stacked = jnp.concatenate([own_ref[...], other_ref[...]], axis=1)
    out_ref[...] = dot(stacked, stacked, ROWS)


def half_gram(own, other):
    w = own.shape[1]
    vmem = pl.BlockSpec(memory_space=pltpu.VMEM)
    return pl.pallas_call(
        gram_kernel,
        in_specs=[vmem, vmem],
        out_specs=vmem,
        out_shape=jax.ShapeDtypeStruct((2 * w, 2 * w), f32),
        compiler_params=pltpu.CompilerParams(vmem_limit_bytes=8 << 20),
    )(own, other)


def pack_kernel(core_ref, after_ref, gram_ref, out_ref):
    w = gram_ref.shape[0] // 2
    even = core_ref[0] == 0
    own, other = gram_ref[:w, :w], gram_ref[w:, w:]
    across = jnp.where(even, gram_ref[:w, w:], gram_ref[w:, :w])
    aa, bb = jnp.where(even, own, other), jnp.where(even, other, own)
    row = lax.broadcasted_iota(jnp.int32, (w, w), 0)
    column = lax.broadcasted_iota(jnp.int32, (w, w), 1)
    shared = jnp.where(row <= column, aa, bb)
    diag = jnp.sum(jnp.where(row == column, bb, 0.0), axis=0, keepdims=True)
    slices, pairs = out_ref.shape[:2]
    each = w // slices
    for k in range(slices):
        for p in range(each // 2):
            first = k * each + 2 * p
            out_ref[k, p] = shared[first : first + 2]
            out_ref[k, each // 2 + p] = across[first : first + 2]
        out_ref[k, pairs - 1] = jnp.broadcast_to(diag, (2, w))


def pack(core, gram, slices, after):
    w = gram.shape[0] // 2
    vmem = pl.BlockSpec(memory_space=pltpu.VMEM)
    return pl.pallas_call(
        pack_kernel,
        in_specs=[
            pl.BlockSpec(memory_space=pltpu.SMEM),
            pl.BlockSpec(memory_space=pl.ANY),
            vmem,
        ],
        out_specs=vmem,
        out_shape=jax.ShapeDtypeStruct((slices, w // slices + 1, 2, w), f32),
        compiler_params=pltpu.CompilerParams(vmem_limit_bytes=4 << 20),
    )(core, after, gram)


def sum_over_chips(part):
    near, far = ("core", "z_lo", "x"), "z_hi"
    n, m = part.shape[0], lax.axis_size(far)
    turned = [[(i + m // 2) % m for i in range(m)]]
    part = lax.all_to_all(part, near, 0, 0)
    part = jnp.broadcast_to(jnp.sum(part, axis=0)[None], (m, *part.shape[1:]))
    part = lax.all_to_all(part, far, 0, 0, axis_index_groups=turned)
    part = jnp.broadcast_to(jnp.sum(part, axis=0)[None], (n, *part.shape[1:]))
    return lax.all_to_all(part, near, 0, 0)


def local(bases, sing_values):
    rows = bases.shape[1]
    points = rows * math.prod(lax.axis_size(axis) for axis in ("z_hi", "z_lo", "x"))
    core = lax.axis_index("core").astype(jnp.int32)

    def partners(value):
        return lax.ppermute(value, "core", [(0, 1), (1, 0)])

    bases = pltpu.with_memory_space_constraint(bases[0], pltpu.HBM)
    sing_values = pltpu.with_memory_space_constraint(sing_values, pltpu.HBM)
    theirs, mine = weigh(core[None], sing_values, bases)
    other_a = partners(theirs)
    other_b = partners(mine)
    slices = math.prod(lax.axis_size(axis) for axis in ("core", "z_lo", "x"))
    blocks = sum_over_chips(pack(core[None], half_gram(mine, other_a), slices, other_b))
    merged, values = finish(
        core[None], blocks, sing_values, bases, other_a, other_b, points
    )
    return (merged[None], values)


def solution(mesh):
    fine = Mesh(mesh.devices.reshape(-1, 2, 8, 2, 4), ("y", "core", "z_hi", "z_lo", "x"))
    specs = (P(("y", "core"), ("z_hi", "z_lo", "x"), None), P(("y", "core"), None))
    return jax.shard_map(local, mesh=fine, in_specs=specs, out_specs=specs, check_vma=False)
```

```python
import functools
import math

import jax
import jax.numpy as jnp
from jax import lax
from jax.experimental import pallas as pl
from jax.experimental.pallas import tpu as pltpu
from jax.sharding import Mesh, PartitionSpec as P

ITERS = 3
NS_STEPS = 6
CHUNK = 1024
ROWS = (((0,), (0,)), ((), ()))
PLAIN = (((1,), (0,)), ((), ()))
COLUMNS = (((1,), (1,)), ((), ()))
bf16 = jnp.bfloat16
f32 = jnp.float32


def dot(a, b, dims=PLAIN):
    return lax.dot_general(a, b, dims, preferred_element_type=f32)


def split(x):
    high = x.astype(bf16)
    return high, (x - high.astype(f32)).astype(bf16)


def wide_dot(a, b, dims=PLAIN):
    (a_high, a_low), (b_high, b_low) = split(a), split(b)
    left = jnp.concatenate([a_high, a_low, a_high], axis=1)
    right = jnp.concatenate([b_high, b_high, b_low], axis=0 if dims is PLAIN else 1)
    return dot(left, right, dims)


def polar_iterate(gram):
    w = gram.shape[0] // 2
    diag = lax.broadcasted_iota(jnp.int32, (w, w), 0) == lax.broadcasted_iota(jnp.int32, (w, w), 1)
    yt = (gram[:w] + gram[w:]) * f32(1.0 / math.sqrt(2.0))
    for outer in range(ITERS):
        scale = 1.0 / (jnp.sum(yt * yt) + 1e-06)
        m = wide_dot(yt, yt, COLUMNS) * scale
        yt = yt * jnp.sqrt(scale)
        last = outer == ITERS - 1
        ahead = yt.T if last else wide_dot(yt, gram)
        square = wide_dot(m, m)
        q = 1.5 * diag.astype(f32) - 0.5 * m
        for inner in range(1, NS_STEPS):
            m = 2.25 * m - 1.5 * square + 0.25 * wide_dot(square, m)
            if inner < NS_STEPS - 1:
                both = wide_dot(jnp.concatenate([m, q], axis=0), m)
                square = both[:w]
                q = 1.5 * q - 0.5 * both[w:]
        u = wide_dot(ahead, q) if last else wide_dot(q, ahead)
        yt = 1.5 * u - 0.5 * (wide_dot(u, m) if last else wide_dot(m, u))
    return yt


def column_squares(gram, rotation):
    high, rest = split(gram)
    low = (gram - high.astype(f32) - rest.astype(f32)).astype(bf16)
    turned = dot(high, rotation) + (dot(rest, rotation) + dot(low, rotation))
    return jnp.sum(turned * rotation.astype(f32), axis=0, keepdims=True)


def weighted(rows, weights_ref):
    return (rows.astype(f32) * weights_ref[...]).astype(bf16)


def finish_kernel(
    points, core_ref, gram_ref, other_weights_ref, weights_hbm, bases_ref, others_ref,
    out_ref, values_ref, gram_rows_ref, weights_ref, own_ref, other_ref, rows_ref, sem, out_sem,
):
    core = core_ref[0]
    rows, w = own_ref.shape
    loads = [
        pltpu.make_async_copy(bases_ref, own_ref, sem.at[0]),
        pltpu.make_async_copy(others_ref, other_ref, sem.at[1]),
        pltpu.make_async_copy(weights_hbm, weights_ref, sem.at[2]),
    ]
    for load in loads:
        load.start()
    slices, pairs = gram_ref.shape[:2]
    each = w // slices
    for k in range(slices):
        for p in range(pairs - 1):
            first = k * each + 2 * p if 2 * p < each else w + k * each + 2 * p - each
            gram_rows_ref[first : first + 2] = gram_ref[k, p]
    shared, ab = gram_rows_ref[:w], gram_rows_ref[w:]
    turned = shared.T
    row = lax.broadcasted_iota(jnp.int32, (w, w), 0)
    column = lax.broadcasted_iota(jnp.int32, (w, w), 1)
    aa = jnp.where(row <= column, shared, turned)
    bb = jnp.where(row > column, shared, jnp.where(row < column, turned, gram_ref[0, pairs - 1, :1]))
    gram = jnp.concatenate(
        [jnp.concatenate([aa, ab], axis=1), jnp.concatenate([ab.T, bb], axis=1)], axis=0
    )
    rotation = polar_iterate(gram).astype(bf16)
    squares = column_squares(gram, rotation)
    values = jnp.sqrt(jnp.maximum(squares, 0.0) / points + 1e-06)
    values_ref[...] = values
    inverse = 1.0 / values
    swapped = jnp.concatenate([rotation[w:], rotation[:w]], axis=0)
    rotation = jnp.where(core == 0, rotation, swapped)
    for load in loads:
        load.wait()
    copies = []
    for j in range(rows // CHUNK):
        part = pl.ds(j * CHUNK, CHUNK)
        own = weighted(own_ref[part], weights_ref)
        stacked = jnp.concatenate([own, weighted(other_ref[part], other_weights_ref)], axis=1)
        rows_ref[part] = (dot(stacked, rotation) * inverse).astype(bf16)
        copies.append(pltpu.make_async_copy(rows_ref.at[part], out_ref.at[part], out_sem.at[j]))
        copies[-1].start()
    for copy in copies:
        copy.wait()


def finish(core, blocks, other_values, sing_values, bases, others, points):
    rows, w = bases.shape
    smem, vmem, hbm, anywhere = (
        pl.BlockSpec(memory_space=space) for space in (pltpu.SMEM, pltpu.VMEM, pltpu.HBM, pl.ANY)
    )
    return pl.pallas_call(
        functools.partial(finish_kernel, points),
        in_specs=[smem, vmem, vmem, hbm, hbm, anywhere],
        out_specs=[anywhere, vmem],
        out_shape=[jax.ShapeDtypeStruct((rows, w), bf16), jax.ShapeDtypeStruct((1, w), f32)],
        scratch_shapes=[
            pltpu.VMEM((2 * w, w), f32),
            pltpu.VMEM(sing_values.shape, f32),
            pltpu.VMEM((rows, w), bf16),
            pltpu.VMEM((rows, w), bf16),
            pltpu.VMEM((rows, w), bf16),
            pltpu.SemaphoreType.DMA((3,)),
            pltpu.SemaphoreType.DMA((rows // CHUNK,)),
        ],
        compiler_params=pltpu.CompilerParams(vmem_limit_bytes=16 << 20),
    )(core, blocks, other_values, sing_values, bases, others)


def weigh_kernel(core_ref, weights_hbm, bases_ref, out_ref, weights_ref, rows_ref, sem):
    half = out_ref.shape[0]
    steps = half // CHUNK
    weights = pltpu.make_async_copy(weights_hbm, weights_ref, sem.at[steps])
    weights.start()
    copies = []
    for j in range(steps):
        first = pl.multiple_of((core_ref[0] * steps + j) * CHUNK, CHUNK)
        here = rows_ref.at[pl.ds(j * CHUNK, CHUNK)]
        copies.append(pltpu.make_async_copy(bases_ref.at[pl.ds(first, CHUNK)], here, sem.at[j]))
        copies[-1].start()
    weights.wait()
    for j, copy in enumerate(copies):
        copy.wait()
        part = pl.ds(j * CHUNK, CHUNK)
        out_ref[part] = weighted(rows_ref[part], weights_ref)


def weigh(core, sing_values, bases):
    rows, w = bases.shape
    vmem, hbm = (pl.BlockSpec(memory_space=space) for space in (pltpu.VMEM, pltpu.HBM))
    return pl.pallas_call(
        weigh_kernel,
        in_specs=[pl.BlockSpec(memory_space=pltpu.SMEM), hbm, hbm],
        out_specs=vmem,
        out_shape=pltpu.VMEM((rows // 2, w), bf16),
        scratch_shapes=[
            pltpu.VMEM(sing_values.shape, f32),
            pltpu.VMEM((rows // 2, w), bf16),
            pltpu.SemaphoreType.DMA((rows // 2 // CHUNK + 1,)),
        ],
        compiler_params=pltpu.CompilerParams(vmem_limit_bytes=8 << 20),
    )(core, sing_values, bases)


def gram_kernel(core_ref, own_ref, others_ref, other_weights_ref, out_ref):
    half, w = own_ref.shape
    first = pl.multiple_of(core_ref[0] * half, half)
    other = weighted(others_ref[pl.ds(first, half)], other_weights_ref)
    stacked = jnp.concatenate([own_ref[...], other], axis=1)
    gram = dot(stacked, stacked, ROWS)
    even = core_ref[0] == 0
    own, other = gram[:w, :w], gram[w:, w:]
    across = jnp.where(even, gram[:w, w:], gram[w:, :w])
    aa, bb = jnp.where(even, own, other), jnp.where(even, other, own)
    row = lax.broadcasted_iota(jnp.int32, (w, w), 0)
    column = lax.broadcasted_iota(jnp.int32, (w, w), 1)
    shared = jnp.where(row <= column, aa, bb)
    diag = jnp.sum(jnp.where(row == column, bb, 0.0), axis=0, keepdims=True)
    slices, pairs = out_ref.shape[:2]
    each = w // slices
    for k in range(slices):
        for p in range(each // 2):
            first = k * each + 2 * p
            out_ref[k, p] = shared[first : first + 2]
            out_ref[k, each // 2 + p] = across[first : first + 2]
        out_ref[k, pairs - 1] = jnp.broadcast_to(diag, (2, w))


def half_gram(core, own, others, other_values, slices):
    w = own.shape[1]
    vmem = pl.BlockSpec(memory_space=pltpu.VMEM)
    return pl.pallas_call(
        gram_kernel,
        in_specs=[pl.BlockSpec(memory_space=pltpu.SMEM)] + [vmem] * 3,
        out_specs=vmem,
        out_shape=jax.ShapeDtypeStruct((slices, w // slices + 1, 2, w), f32),
        compiler_params=pltpu.CompilerParams(vmem_limit_bytes=12 << 20),
    )(core, own, others, other_values)


def sum_over_chips(part):
    near, far = ("core", "z_lo", "x"), "z_hi"
    n, m = part.shape[0], lax.axis_size(far)
    turned = [[(i + m // 2) % m for i in range(m)]]
    part = lax.all_to_all(part, near, 0, 0)
    part = jnp.broadcast_to(jnp.sum(part, axis=0)[None], (m, *part.shape[1:]))
    part = lax.all_to_all(part, far, 0, 0, axis_index_groups=turned)
    part = jnp.broadcast_to(jnp.sum(part, axis=0)[None], (n, *part.shape[1:]))
    return lax.all_to_all(part, near, 0, 0)


def local(bases, sing_values):
    rows = bases.shape[1]
    points = rows * math.prod(lax.axis_size(axis) for axis in ("z_hi", "z_lo", "x"))
    core = lax.axis_index("core").astype(jnp.int32)

    def partners(value):
        return lax.ppermute(value, "core", [(0, 1), (1, 0)])

    others, other_values = partners(bases[0]), partners(sing_values)
    bases = pltpu.with_memory_space_constraint(bases[0], pltpu.HBM)
    sing_values = pltpu.with_memory_space_constraint(sing_values, pltpu.HBM)
    mine = weigh(core[None], sing_values, bases)
    slices = math.prod(lax.axis_size(axis) for axis in ("core", "z_lo", "x"))
    blocks = sum_over_chips(half_gram(core[None], mine, others, other_values, slices))
    merged, values = finish(core[None], blocks, other_values, sing_values, bases, others, points)
    return (merged[None], values)


def solution(mesh):
    fine = Mesh(mesh.devices.reshape(-1, 2, 8, 2, 4), ("y", "core", "z_hi", "z_lo", "x"))
    specs = (P(("y", "core"), ("z_hi", "z_lo", "x"), None), P(("y", "core"), None))
    return jax.shard_map(local, mesh=fine, in_specs=specs, out_specs=specs, check_vma=False)
```

```python
import functools
import math

import jax
import jax.numpy as jnp
from jax import lax
from jax.experimental import pallas as pl
from jax.experimental.pallas import tpu as pltpu
from jax.sharding import Mesh, PartitionSpec as P

ITERS = 3
NS_STEPS = 6
CHUNK = 1024
FIRST = 10
ROWS = (((0,), (0,)), ((), ()))
PLAIN = (((1,), (0,)), ((), ()))
COLUMNS = (((1,), (1,)), ((), ()))
bf16 = jnp.bfloat16
f32 = jnp.float32


def dot(a, b, dims=PLAIN):
    return lax.dot_general(a, b, dims, preferred_element_type=f32)


def split(x):
    high = x.astype(bf16)
    return high, (x - high.astype(f32)).astype(bf16)


def wide_dot(a, b, dims=PLAIN):
    (a_high, a_low), (b_high, b_low) = split(a), split(b)
    left = jnp.concatenate([a_high, a_low, a_high], axis=1)
    right = jnp.concatenate([b_high, b_high, b_low], axis=0 if dims is PLAIN else 1)
    return dot(left, right, dims)


def polar_iterate(gram):
    w = gram.shape[0] // 2
    diag = lax.broadcasted_iota(jnp.int32, (w, w), 0) == lax.broadcasted_iota(jnp.int32, (w, w), 1)
    yt = (gram[:w] + gram[w:]) * f32(1.0 / math.sqrt(2.0))
    for outer in range(ITERS):
        scale = 1.0 / (jnp.sum(yt * yt) + 1e-06)
        m = wide_dot(yt, yt, COLUMNS) * scale
        yt = yt * jnp.sqrt(scale)
        last = outer == ITERS - 1
        ahead = yt.T if last else wide_dot(yt, gram)
        square = wide_dot(m, m)
        q = 1.5 * diag.astype(f32) - 0.5 * m
        for inner in range(1, NS_STEPS):
            m = 2.25 * m - 1.5 * square + 0.25 * wide_dot(square, m)
            if inner < NS_STEPS - 1:
                both = wide_dot(jnp.concatenate([m, q], axis=0), m)
                square = both[:w]
                q = 1.5 * q - 0.5 * both[w:]
        u = wide_dot(ahead, q) if last else wide_dot(q, ahead)
        yt = 1.5 * u - 0.5 * (wide_dot(u, m) if last else wide_dot(m, u))
    return yt


def column_squares(gram, rotation):
    high, rest = split(gram)
    low = (gram - high.astype(f32) - rest.astype(f32)).astype(bf16)
    turned = dot(high, rotation) + (dot(rest, rotation) + dot(low, rotation))
    return jnp.sum(turned * rotation.astype(f32), axis=0, keepdims=True)


def weighted(rows, weights_ref):
    return (rows.astype(f32) * weights_ref[...]).astype(bf16)


def finish_kernel(
    points, core_ref, gram_ref, other_weights_ref, weights_hbm, bases_ref, others_ref,
    out_ref, values_ref, gram_rows_ref, weights_ref, own_ref, other_ref, rows_ref, sem, out_sem,
):
    core = core_ref[0]
    rows, w = own_ref.shape
    loads = [
        pltpu.make_async_copy(bases_ref, own_ref, sem.at[0]),
        pltpu.make_async_copy(others_ref, other_ref, sem.at[1]),
        pltpu.make_async_copy(weights_hbm, weights_ref, sem.at[2]),
    ]
    for load in loads:
        load.start()
    slices, pairs = gram_ref.shape[:2]
    each = w // slices
    for k in range(slices):
        for p in range(pairs - 1):
            first = k * each + 2 * p if 2 * p < each else w + k * each + 2 * p - each
            gram_rows_ref[first : first + 2] = gram_ref[k, p]
    shared, ab = gram_rows_ref[:w], gram_rows_ref[w:]
    turned = shared.T
    row = lax.broadcasted_iota(jnp.int32, (w, w), 0)
    column = lax.broadcasted_iota(jnp.int32, (w, w), 1)
    aa = jnp.where(row <= column, shared, turned)
    bb = jnp.where(row > column, shared, jnp.where(row < column, turned, gram_ref[0, pairs - 1, :1]))
    gram = jnp.concatenate(
        [jnp.concatenate([aa, ab], axis=1), jnp.concatenate([ab.T, bb], axis=1)], axis=0
    )
    rotation = polar_iterate(gram).astype(bf16)
    for load in loads:
        load.wait()
    squares = column_squares(gram, rotation)
    values = jnp.sqrt(jnp.maximum(squares, 0.0) / points + 1e-06)
    values_ref[...] = values
    inverse = 1.0 / values
    swapped = jnp.concatenate([rotation[w:], rotation[:w]], axis=0)
    rotation = jnp.where(core == 0, rotation, swapped)
    copies = []
    for j in range(rows // CHUNK):
        part = pl.ds(j * CHUNK, CHUNK)
        own = weighted(own_ref[part], weights_ref)
        stacked = jnp.concatenate([own, weighted(other_ref[part], other_weights_ref)], axis=1)
        rows_ref[part] = (dot(stacked, rotation) * inverse).astype(bf16)
        copies.append(pltpu.make_async_copy(rows_ref.at[part], out_ref.at[part], out_sem.at[j]))
        copies[-1].start()
    for copy in copies:
        copy.wait()


def finish(core, blocks, other_values, sing_values, bases, others, points):
    rows, w = bases.shape
    smem, vmem, hbm, anywhere = (
        pl.BlockSpec(memory_space=space) for space in (pltpu.SMEM, pltpu.VMEM, pltpu.HBM, pl.ANY)
    )
    return pl.pallas_call(
        functools.partial(finish_kernel, points),
        in_specs=[smem, vmem, vmem, hbm, hbm, anywhere],
        out_specs=[anywhere, vmem],
        out_shape=[jax.ShapeDtypeStruct((rows, w), bf16), jax.ShapeDtypeStruct((1, w), f32)],
        scratch_shapes=[
            pltpu.VMEM((2 * w, w), f32),
            pltpu.VMEM(sing_values.shape, f32),
            pltpu.VMEM((rows, w), bf16),
            pltpu.VMEM((rows, w), bf16),
            pltpu.VMEM((rows, w), bf16),
            pltpu.SemaphoreType.DMA((3,)),
            pltpu.SemaphoreType.DMA((rows // CHUNK,)),
        ],
        compiler_params=pltpu.CompilerParams(vmem_limit_bytes=16 << 20),
    )(core, blocks, other_values, sing_values, bases, others)


def weigh_kernel(core_ref, weights_hbm, bases_ref, out_ref, weights_ref, rows_ref, sem):
    half = out_ref.shape[0]
    steps = half // CHUNK
    weights = pltpu.make_async_copy(weights_hbm, weights_ref, sem.at[steps])
    weights.start()
    copies = []
    for j in range(steps):
        first = pl.multiple_of((core_ref[0] * steps + j) * CHUNK, CHUNK)
        here = rows_ref.at[pl.ds(j * CHUNK, CHUNK)]
        copies.append(pltpu.make_async_copy(bases_ref.at[pl.ds(first, CHUNK)], here, sem.at[j]))
        copies[-1].start()
    weights.wait()
    for j, copy in enumerate(copies):
        copy.wait()
        part = pl.ds(j * CHUNK, CHUNK)
        out_ref[part] = weighted(rows_ref[part], weights_ref)


def weigh(core, sing_values, bases):
    rows, w = bases.shape
    vmem, hbm = (pl.BlockSpec(memory_space=space) for space in (pltpu.VMEM, pltpu.HBM))
    return pl.pallas_call(
        weigh_kernel,
        in_specs=[pl.BlockSpec(memory_space=pltpu.SMEM), hbm, hbm],
        out_specs=vmem,
        out_shape=pltpu.VMEM((rows // 2, w), bf16),
        scratch_shapes=[
            pltpu.VMEM(sing_values.shape, f32),
            pltpu.VMEM((rows // 2, w), bf16),
            pltpu.SemaphoreType.DMA((rows // 2 // CHUNK + 1,)),
        ],
        compiler_params=pltpu.CompilerParams(vmem_limit_bytes=8 << 20),
    )(core, sing_values, bases)


def gram_kernel(core_ref, own_ref, others_ref, other_weights_ref, out_ref):
    half, w = own_ref.shape
    first = pl.multiple_of(core_ref[0] * half, half)
    other = weighted(others_ref[pl.ds(first, half)], other_weights_ref)
    stacked = jnp.concatenate([own_ref[...], other], axis=1)
    gram = dot(stacked, stacked, ROWS)
    even = core_ref[0] == 0
    own, other = gram[:w, :w], gram[w:, w:]
    across = jnp.where(even, gram[:w, w:], gram[w:, :w])
    aa, bb = jnp.where(even, own, other), jnp.where(even, other, own)
    row = lax.broadcasted_iota(jnp.int32, (w, w), 0)
    column = lax.broadcasted_iota(jnp.int32, (w, w), 1)
    shared = jnp.where(row <= column, aa, bb)
    diag = jnp.sum(jnp.where(row == column, bb, 0.0), axis=0, keepdims=True)
    slices, pairs = out_ref.shape[:2]
    each = w // slices
    for k in range(slices):
        for p in range(each // 2):
            first = k * each + 2 * p
            out_ref[(k - FIRST) % slices, p] = shared[first : first + 2]
            out_ref[(k - FIRST) % slices, each // 2 + p] = across[first : first + 2]
        out_ref[k, pairs - 1] = jnp.broadcast_to(diag, (2, w))


def half_gram(core, own, others, other_values, slices):
    w = own.shape[1]
    vmem = pl.BlockSpec(memory_space=pltpu.VMEM)
    return pl.pallas_call(
        gram_kernel,
        in_specs=[pl.BlockSpec(memory_space=pltpu.SMEM)] + [vmem] * 3,
        out_specs=vmem,
        out_shape=jax.ShapeDtypeStruct((slices, w // slices + 1, 2, w), f32),
        compiler_params=pltpu.CompilerParams(vmem_limit_bytes=12 << 20),
    )(core, own, others, other_values)


def sum_over_chips(part):
    near, far = ("core", "z_lo", "x"), "z_hi"
    n, m = part.shape[0], lax.axis_size(far)
    turned = [[(i + m // 2) % m for i in range(m)]]
    near_turned = [[(i + FIRST) % n for i in range(n)]]
    part = lax.all_to_all(part, near, 0, 0, axis_index_groups=near_turned)
    part = jnp.broadcast_to(jnp.sum(part, axis=0)[None], (m, *part.shape[1:]))
    part = lax.all_to_all(part, far, 0, 0, axis_index_groups=turned)
    part = jnp.broadcast_to(jnp.sum(part, axis=0)[None], (n, *part.shape[1:]))
    return lax.all_to_all(part, near, 0, 0)


def local(bases, sing_values):
    rows = bases.shape[1]
    points = rows * math.prod(lax.axis_size(axis) for axis in ("z_hi", "z_lo", "x"))
    core = lax.axis_index("core").astype(jnp.int32)

    def partners(value):
        return lax.ppermute(value, "core", [(0, 1), (1, 0)])

    others, other_values = partners(bases[0]), partners(sing_values)
    bases = pltpu.with_memory_space_constraint(bases[0], pltpu.HBM)
    sing_values = pltpu.with_memory_space_constraint(sing_values, pltpu.HBM)
    mine = weigh(core[None], sing_values, bases)
    slices = math.prod(lax.axis_size(axis) for axis in ("core", "z_lo", "x"))
    blocks = sum_over_chips(half_gram(core[None], mine, others, other_values, slices))
    merged, values = finish(core[None], blocks, other_values, sing_values, bases, others, points)
    return (merged[None], values)


def solution(mesh):
    fine = Mesh(mesh.devices.reshape(-1, 2, 8, 2, 4), ("y", "core", "z_hi", "z_lo", "x"))
    specs = (P(("y", "core"), ("z_hi", "z_lo", "x"), None), P(("y", "core"), None))
    return jax.shard_map(local, mesh=fine, in_specs=specs, out_specs=specs, check_vma=False)
```

```python
import functools
import math

import jax
import jax.numpy as jnp
from jax import lax
from jax.experimental import pallas as pl
from jax.experimental.pallas import tpu as pltpu
from jax.sharding import Mesh, PartitionSpec as P

ITERS = 3
NS_STEPS = 6
CHUNK = 1024
FIRST = 10
FAR_FIRST = 5
GATHER_FIRST = 14
ROWS = (((0,), (0,)), ((), ()))
PLAIN = (((1,), (0,)), ((), ()))
COLUMNS = (((1,), (1,)), ((), ()))
bf16 = jnp.bfloat16
f32 = jnp.float32


def dot(a, b, dims=PLAIN):
    return lax.dot_general(a, b, dims, preferred_element_type=f32)


def split(x):
    high = x.astype(bf16)
    return high, (x - high.astype(f32)).astype(bf16)


def wide_dot(a, b, dims=PLAIN):
    (a_high, a_low), (b_high, b_low) = split(a), split(b)
    left = jnp.concatenate([a_high, a_low, a_high], axis=1)
    right = jnp.concatenate([b_high, b_high, b_low], axis=0 if dims is PLAIN else 1)
    return dot(left, right, dims)


def polar_iterate(gram):
    w = gram.shape[0] // 2
    diag = lax.broadcasted_iota(jnp.int32, (w, w), 0) == lax.broadcasted_iota(jnp.int32, (w, w), 1)
    yt = (gram[:w] + gram[w:]) * f32(1.0 / math.sqrt(2.0))
    for outer in range(ITERS):
        scale = 1.0 / (jnp.sum(yt * yt) + 1e-06)
        m = wide_dot(yt, yt, COLUMNS) * scale
        yt = yt * jnp.sqrt(scale)
        last = outer == ITERS - 1
        ahead = yt.T if last else wide_dot(yt, gram)
        square = wide_dot(m, m)
        q = 1.5 * diag.astype(f32) - 0.5 * m
        for inner in range(1, NS_STEPS):
            m = 2.25 * m - 1.5 * square + 0.25 * wide_dot(square, m)
            if inner < NS_STEPS - 1:
                both = wide_dot(jnp.concatenate([m, q], axis=0), m)
                square = both[:w]
                q = 1.5 * q - 0.5 * both[w:]
        u = wide_dot(ahead, q) if last else wide_dot(q, ahead)
        yt = 1.5 * u - 0.5 * (wide_dot(u, m) if last else wide_dot(m, u))
    return yt


def column_squares(gram, rotation):
    high, rest = split(gram)
    low = (gram - high.astype(f32) - rest.astype(f32)).astype(bf16)
    turned = dot(high, rotation) + (dot(rest, rotation) + dot(low, rotation))
    return jnp.sum(turned * rotation.astype(f32), axis=0, keepdims=True)


def weighted(rows, weights_ref):
    return (rows.astype(f32) * weights_ref[...]).astype(bf16)


def finish_kernel(
    points, core_ref, gram_ref, other_weights_ref, weights_hbm, bases_ref, others_ref,
    out_ref, values_ref, gram_rows_ref, weights_ref, own_ref, other_ref, rows_ref, sem, out_sem,
):
    core = core_ref[0]
    rows, w = own_ref.shape
    loads = [
        pltpu.make_async_copy(bases_ref, own_ref, sem.at[0]),
        pltpu.make_async_copy(others_ref, other_ref, sem.at[1]),
        pltpu.make_async_copy(weights_hbm, weights_ref, sem.at[2]),
    ]
    for load in loads:
        load.start()
    slices, pairs = gram_ref.shape[:2]
    each = w // slices
    for k in range(slices):
        for p in range(pairs - 1):
            first = k * each + 2 * p if 2 * p < each else w + k * each + 2 * p - each
            gram_rows_ref[first : first + 2] = gram_ref[(k - GATHER_FIRST) % slices, p]
    shared, ab = gram_rows_ref[:w], gram_rows_ref[w:]
    turned = shared.T
    row = lax.broadcasted_iota(jnp.int32, (w, w), 0)
    column = lax.broadcasted_iota(jnp.int32, (w, w), 1)
    aa = jnp.where(row <= column, shared, turned)
    bb = jnp.where(row > column, shared, jnp.where(row < column, turned, gram_ref[0, pairs - 1, :1]))
    gram = jnp.concatenate(
        [jnp.concatenate([aa, ab], axis=1), jnp.concatenate([ab.T, bb], axis=1)], axis=0
    )
    rotation = polar_iterate(gram).astype(bf16)
    for load in loads:
        load.wait()
    squares = column_squares(gram, rotation)
    values = jnp.sqrt(jnp.maximum(squares, 0.0) / points + 1e-06)
    values_ref[...] = values
    inverse = 1.0 / values
    swapped = jnp.concatenate([rotation[w:], rotation[:w]], axis=0)
    rotation = jnp.where(core == 0, rotation, swapped)
    copies = []
    for j in range(rows // CHUNK):
        part = pl.ds(j * CHUNK, CHUNK)
        own = weighted(own_ref[part], weights_ref)
        stacked = jnp.concatenate([own, weighted(other_ref[part], other_weights_ref)], axis=1)
        rows_ref[part] = (dot(stacked, rotation) * inverse).astype(bf16)
        copies.append(pltpu.make_async_copy(rows_ref.at[part], out_ref.at[part], out_sem.at[j]))
        copies[-1].start()
    for copy in copies:
        copy.wait()


def finish(core, blocks, other_values, sing_values, bases, others, points):
    rows, w = bases.shape
    smem, vmem, hbm, anywhere = (
        pl.BlockSpec(memory_space=space) for space in (pltpu.SMEM, pltpu.VMEM, pltpu.HBM, pl.ANY)
    )
    return pl.pallas_call(
        functools.partial(finish_kernel, points),
        in_specs=[smem, vmem, vmem, hbm, hbm, anywhere],
        out_specs=[anywhere, vmem],
        out_shape=[jax.ShapeDtypeStruct((rows, w), bf16), jax.ShapeDtypeStruct((1, w), f32)],
        scratch_shapes=[
            pltpu.VMEM((2 * w, w), f32),
            pltpu.VMEM(sing_values.shape, f32),
            pltpu.VMEM((rows, w), bf16),
            pltpu.VMEM((rows, w), bf16),
            pltpu.VMEM((rows, w), bf16),
            pltpu.SemaphoreType.DMA((3,)),
            pltpu.SemaphoreType.DMA((rows // CHUNK,)),
        ],
        compiler_params=pltpu.CompilerParams(vmem_limit_bytes=16 << 20),
    )(core, blocks, other_values, sing_values, bases, others)


def weigh_kernel(core_ref, weights_hbm, bases_ref, out_ref, weights_ref, rows_ref, sem):
    half = out_ref.shape[0]
    steps = half // CHUNK
    weights = pltpu.make_async_copy(weights_hbm, weights_ref, sem.at[steps])
    weights.start()
    copies = []
    for j in range(steps):
        first = pl.multiple_of((core_ref[0] * steps + j) * CHUNK, CHUNK)
        here = rows_ref.at[pl.ds(j * CHUNK, CHUNK)]
        copies.append(pltpu.make_async_copy(bases_ref.at[pl.ds(first, CHUNK)], here, sem.at[j]))
        copies[-1].start()
    weights.wait()
    for j, copy in enumerate(copies):
        copy.wait()
        part = pl.ds(j * CHUNK, CHUNK)
        out_ref[part] = weighted(rows_ref[part], weights_ref)


def weigh(core, sing_values, bases):
    rows, w = bases.shape
    vmem, hbm = (pl.BlockSpec(memory_space=space) for space in (pltpu.VMEM, pltpu.HBM))
    return pl.pallas_call(
        weigh_kernel,
        in_specs=[pl.BlockSpec(memory_space=pltpu.SMEM), hbm, hbm],
        out_specs=vmem,
        out_shape=pltpu.VMEM((rows // 2, w), bf16),
        scratch_shapes=[
            pltpu.VMEM(sing_values.shape, f32),
            pltpu.VMEM((rows // 2, w), bf16),
            pltpu.SemaphoreType.DMA((rows // 2 // CHUNK + 1,)),
        ],
        compiler_params=pltpu.CompilerParams(vmem_limit_bytes=8 << 20),
    )(core, sing_values, bases)


def gram_kernel(core_ref, own_ref, others_ref, other_weights_ref, out_ref):
    half, w = own_ref.shape
    first = pl.multiple_of(core_ref[0] * half, half)
    other = weighted(others_ref[pl.ds(first, half)], other_weights_ref)
    stacked = jnp.concatenate([own_ref[...], other], axis=1)
    gram = dot(stacked, stacked, ROWS)
    even = core_ref[0] == 0
    own, other = gram[:w, :w], gram[w:, w:]
    across = jnp.where(even, gram[:w, w:], gram[w:, :w])
    aa, bb = jnp.where(even, own, other), jnp.where(even, other, own)
    row = lax.broadcasted_iota(jnp.int32, (w, w), 0)
    column = lax.broadcasted_iota(jnp.int32, (w, w), 1)
    shared = jnp.where(row <= column, aa, bb)
    diag = jnp.sum(jnp.where(row == column, bb, 0.0), axis=0, keepdims=True)
    slices, pairs = out_ref.shape[:2]
    each = w // slices
    for k in range(slices):
        for p in range(each // 2):
            first = k * each + 2 * p
            out_ref[(k - FIRST) % slices, p] = shared[first : first + 2]
            out_ref[(k - FIRST) % slices, each // 2 + p] = across[first : first + 2]
        out_ref[k, pairs - 1] = jnp.broadcast_to(diag, (2, w))


def half_gram(core, own, others, other_values, slices):
    w = own.shape[1]
    vmem = pl.BlockSpec(memory_space=pltpu.VMEM)
    return pl.pallas_call(
        gram_kernel,
        in_specs=[pl.BlockSpec(memory_space=pltpu.SMEM)] + [vmem] * 3,
        out_specs=vmem,
        out_shape=jax.ShapeDtypeStruct((slices, w // slices + 1, 2, w), f32),
        compiler_params=pltpu.CompilerParams(vmem_limit_bytes=12 << 20),
    )(core, own, others, other_values)


def sum_over_chips(part):
    near, far = ("core", "z_lo", "x"), "z_hi"
    n, m = part.shape[0], lax.axis_size(far)

    def turned(size, first):
        return [[(i + first) % size for i in range(size)]]

    part = lax.all_to_all(part, near, 0, 0, axis_index_groups=turned(n, FIRST))
    part = jnp.broadcast_to(jnp.sum(part, axis=0)[None], (m, *part.shape[1:]))
    part = lax.all_to_all(part, far, 0, 0, axis_index_groups=turned(m, FAR_FIRST))
    part = jnp.broadcast_to(jnp.sum(part, axis=0)[None], (n, *part.shape[1:]))
    return lax.all_to_all(part, near, 0, 0, axis_index_groups=turned(n, GATHER_FIRST))


def local(bases, sing_values):
    rows = bases.shape[1]
    points = rows * math.prod(lax.axis_size(axis) for axis in ("z_hi", "z_lo", "x"))
    core = lax.axis_index("core").astype(jnp.int32)

    def partners(value):
        return lax.ppermute(value, "core", [(0, 1), (1, 0)])

    others, other_values = partners(bases[0]), partners(sing_values)
    bases = pltpu.with_memory_space_constraint(bases[0], pltpu.HBM)
    sing_values = pltpu.with_memory_space_constraint(sing_values, pltpu.HBM)
    mine = weigh(core[None], sing_values, bases)
    slices = math.prod(lax.axis_size(axis) for axis in ("core", "z_lo", "x"))
    blocks = sum_over_chips(half_gram(core[None], mine, others, other_values, slices))
    merged, values = finish(core[None], blocks, other_values, sing_values, bases, others, points)
    return (merged[None], values)


def solution(mesh):
    fine = Mesh(mesh.devices.reshape(-1, 2, 8, 2, 4), ("y", "core", "z_hi", "z_lo", "x"))
    specs = (P(("y", "core"), ("z_hi", "z_lo", "x"), None), P(("y", "core"), None))
    return jax.shard_map(local, mesh=fine, in_specs=specs, out_specs=specs, check_vma=False)
```

```python
import functools
import math

import jax
import jax.numpy as jnp
from jax import lax
from jax.experimental import pallas as pl
from jax.experimental.pallas import tpu as pltpu
from jax.sharding import Mesh, PartitionSpec as P

ITERS = 3
NS_STEPS = 6
CHUNK = 1024
FIRST = 10
FAR_FIRST = 5
GATHER_FIRST = 14
ROWS = (((0,), (0,)), ((), ()))
PLAIN = (((1,), (0,)), ((), ()))
COLUMNS = (((1,), (1,)), ((), ()))
bf16 = jnp.bfloat16
f32 = jnp.float32


def dot(a, b, dims=PLAIN):
    return lax.dot_general(a, b, dims, preferred_element_type=f32)


def split(x):
    high = x.astype(bf16)
    return high, (x - high.astype(f32)).astype(bf16)


def wide_dot(a, b, dims=PLAIN):
    (a_high, a_low), (b_high, b_low) = split(a), split(b)
    left = jnp.concatenate([a_high, a_low, a_high], axis=1)
    right = jnp.concatenate([b_high, b_high, b_low], axis=0 if dims is PLAIN else 1)
    return dot(left, right, dims)


def polar_iterate(gram):
    w = gram.shape[0] // 2
    diag = lax.broadcasted_iota(jnp.int32, (w, w), 0) == lax.broadcasted_iota(jnp.int32, (w, w), 1)
    yt = (gram[:w] + gram[w:]) * f32(1.0 / math.sqrt(2.0))
    for outer in range(ITERS):
        scale = 1.0 / (jnp.sum(yt * yt) + 1e-06)
        m = wide_dot(yt, yt, COLUMNS) * scale
        yt = yt * jnp.sqrt(scale)
        last = outer == ITERS - 1
        ahead = yt.T if last else wide_dot(yt, gram)
        square = wide_dot(m, m)
        q = 1.5 * diag.astype(f32) - 0.5 * m
        for inner in range(1, NS_STEPS):
            m = 2.25 * m - 1.5 * square + 0.25 * wide_dot(square, m)
            if inner < NS_STEPS - 1:
                both = wide_dot(jnp.concatenate([m, q], axis=0), m)
                square = both[:w]
                q = 1.5 * q - 0.5 * both[w:]
        u = wide_dot(ahead, q) if last else wide_dot(q, ahead)
        yt = 1.5 * u - 0.5 * (wide_dot(u, m) if last else wide_dot(m, u))
    return yt


def column_squares(gram, rotation):
    high, rest = split(gram)
    low = (gram - high.astype(f32) - rest.astype(f32)).astype(bf16)
    turned = dot(high, rotation) + (dot(rest, rotation) + dot(low, rotation))
    return jnp.sum(turned * rotation.astype(f32), axis=0, keepdims=True)


def weighted(rows, weights_ref):
    return (rows.astype(f32) * weights_ref[...]).astype(bf16)


def finish_kernel(
    points, core_ref, gram_ref, other_weights_ref, weights_hbm, bases_ref, others_ref,
    out_ref, values_ref, gram_rows_ref, weights_ref, own_ref, other_ref, rows_ref, sem, out_sem,
):
    core = core_ref[0]
    rows, w = own_ref.shape
    loads = [
        pltpu.make_async_copy(bases_ref, own_ref, sem.at[0]),
        pltpu.make_async_copy(others_ref, other_ref, sem.at[1]),
        pltpu.make_async_copy(weights_hbm, weights_ref, sem.at[2]),
    ]
    for load in loads:
        load.start()
    slices, lines = gram_ref.shape[:2]
    each = w // slices
    for k in range(slices):
        for p in range(lines - 1):
            first = k * each + p if p < each else w + k * each + p - each
            gram_rows_ref[first : first + 1] = gram_ref[(k - GATHER_FIRST) % slices, p]
    shared, ab = gram_rows_ref[:w], gram_rows_ref[w:]
    turned = shared.T
    row = lax.broadcasted_iota(jnp.int32, (w, w), 0)
    column = lax.broadcasted_iota(jnp.int32, (w, w), 1)
    aa = jnp.where(row <= column, shared, turned)
    bb = jnp.where(row > column, shared, jnp.where(row < column, turned, gram_ref[0, lines - 1]))
    gram = jnp.concatenate(
        [jnp.concatenate([aa, ab], axis=1), jnp.concatenate([ab.T, bb], axis=1)], axis=0
    )
    rotation = polar_iterate(gram).astype(bf16)
    for load in loads:
        load.wait()
    squares = column_squares(gram, rotation)
    values = jnp.sqrt(jnp.maximum(squares, 0.0) / points + 1e-06)
    values_ref[...] = values
    inverse = 1.0 / values
    swapped = jnp.concatenate([rotation[w:], rotation[:w]], axis=0)
    rotation = jnp.where(core == 0, rotation, swapped)
    copies = []
    for j in range(rows // CHUNK):
        part = pl.ds(j * CHUNK, CHUNK)
        own = weighted(own_ref[part], weights_ref)
        stacked = jnp.concatenate([own, weighted(other_ref[part], other_weights_ref)], axis=1)
        rows_ref[part] = (dot(stacked, rotation) * inverse).astype(bf16)
        copies.append(pltpu.make_async_copy(rows_ref.at[part], out_ref.at[part], out_sem.at[j]))
        copies[-1].start()
    for copy in copies:
        copy.wait()


def finish(core, blocks, other_values, sing_values, bases, others, points):
    rows, w = bases.shape
    smem, vmem, hbm, anywhere = (
        pl.BlockSpec(memory_space=space) for space in (pltpu.SMEM, pltpu.VMEM, pltpu.HBM, pl.ANY)
    )
    return pl.pallas_call(
        functools.partial(finish_kernel, points),
        in_specs=[smem, vmem, vmem, hbm, hbm, anywhere],
        out_specs=[anywhere, vmem],
        out_shape=[jax.ShapeDtypeStruct((rows, w), bf16), jax.ShapeDtypeStruct((1, w), f32)],
        scratch_shapes=[
            pltpu.VMEM((2 * w, w), f32),
            pltpu.VMEM(sing_values.shape, f32),
            pltpu.VMEM((rows, w), bf16),
            pltpu.VMEM((rows, w), bf16),
            pltpu.VMEM((rows, w), bf16),
            pltpu.SemaphoreType.DMA((3,)),
            pltpu.SemaphoreType.DMA((rows // CHUNK,)),
        ],
        compiler_params=pltpu.CompilerParams(vmem_limit_bytes=16 << 20),
    )(core, blocks, other_values, sing_values, bases, others)


def weigh_kernel(core_ref, weights_hbm, bases_ref, out_ref, weights_ref, rows_ref, sem):
    half = out_ref.shape[0]
    steps = half // CHUNK
    weights = pltpu.make_async_copy(weights_hbm, weights_ref, sem.at[steps])
    weights.start()
    copies = []
    for j in range(steps):
        first = pl.multiple_of((core_ref[0] * steps + j) * CHUNK, CHUNK)
        here = rows_ref.at[pl.ds(j * CHUNK, CHUNK)]
        copies.append(pltpu.make_async_copy(bases_ref.at[pl.ds(first, CHUNK)], here, sem.at[j]))
        copies[-1].start()
    weights.wait()
    for j, copy in enumerate(copies):
        copy.wait()
        part = pl.ds(j * CHUNK, CHUNK)
        out_ref[part] = weighted(rows_ref[part], weights_ref)


def weigh(core, sing_values, bases):
    rows, w = bases.shape
    vmem, hbm = (pl.BlockSpec(memory_space=space) for space in (pltpu.VMEM, pltpu.HBM))
    return pl.pallas_call(
        weigh_kernel,
        in_specs=[pl.BlockSpec(memory_space=pltpu.SMEM), hbm, hbm],
        out_specs=vmem,
        out_shape=pltpu.VMEM((rows // 2, w), bf16),
        scratch_shapes=[
            pltpu.VMEM(sing_values.shape, f32),
            pltpu.VMEM((rows // 2, w), bf16),
            pltpu.SemaphoreType.DMA((rows // 2 // CHUNK + 1,)),
        ],
        compiler_params=pltpu.CompilerParams(vmem_limit_bytes=8 << 20),
    )(core, sing_values, bases)


def gram_kernel(core_ref, own_ref, others_ref, other_weights_ref, out_ref):
    half, w = own_ref.shape
    first = pl.multiple_of(core_ref[0] * half, half)
    other = weighted(others_ref[pl.ds(first, half)], other_weights_ref)
    stacked = jnp.concatenate([own_ref[...], other], axis=1)
    gram = dot(stacked, stacked, ROWS)
    even = core_ref[0] == 0
    own, other = gram[:w, :w], gram[w:, w:]
    across = jnp.where(even, gram[:w, w:], gram[w:, :w])
    aa, bb = jnp.where(even, own, other), jnp.where(even, other, own)
    row = lax.broadcasted_iota(jnp.int32, (w, w), 0)
    column = lax.broadcasted_iota(jnp.int32, (w, w), 1)
    shared = jnp.where(row <= column, aa, bb)
    diag = jnp.sum(jnp.where(row == column, bb, 0.0), axis=0, keepdims=True)
    slices, lines = out_ref.shape[:2]
    each = w // slices
    for k in range(slices):
        for p in range(each):
            first = k * each + p
            out_ref[(k - FIRST) % slices, p] = shared[first : first + 1]
            out_ref[(k - FIRST) % slices, each + p] = across[first : first + 1]
        out_ref[k, lines - 1] = diag


def half_gram(core, own, others, other_values, slices):
    w = own.shape[1]
    vmem = pl.BlockSpec(memory_space=pltpu.VMEM)
    return pl.pallas_call(
        gram_kernel,
        in_specs=[pl.BlockSpec(memory_space=pltpu.SMEM)] + [vmem] * 3,
        out_specs=vmem,
        out_shape=jax.ShapeDtypeStruct((slices, 2 * (w // slices) + 1, 1, w), f32),
        compiler_params=pltpu.CompilerParams(vmem_limit_bytes=12 << 20),
    )(core, own, others, other_values)


def sum_over_chips(part):
    near, far = ("core", "z_lo", "x"), "z_hi"
    n, m = part.shape[0], lax.axis_size(far)

    def turned(size, first):
        return [[(i + first) % size for i in range(size)]]

    part = lax.all_to_all(part, near, 0, 0, axis_index_groups=turned(n, FIRST))
    part = jnp.broadcast_to(jnp.sum(part, axis=0)[None], (m, *part.shape[1:]))
    part = lax.all_to_all(part, far, 0, 0, axis_index_groups=turned(m, FAR_FIRST))
    part = jnp.broadcast_to(jnp.sum(part, axis=0)[None], (n, *part.shape[1:]))
    return lax.all_to_all(part, near, 0, 0, axis_index_groups=turned(n, GATHER_FIRST))


def local(bases, sing_values):
    rows = bases.shape[1]
    points = rows * math.prod(lax.axis_size(axis) for axis in ("z_hi", "z_lo", "x"))
    core = lax.axis_index("core").astype(jnp.int32)

    def partners(value):
        return lax.ppermute(value, "core", [(0, 1), (1, 0)])

    others, other_values = partners(bases[0]), partners(sing_values)
    bases = pltpu.with_memory_space_constraint(bases[0], pltpu.HBM)
    sing_values = pltpu.with_memory_space_constraint(sing_values, pltpu.HBM)
    mine = weigh(core[None], sing_values, bases)
    slices = math.prod(lax.axis_size(axis) for axis in ("core", "z_lo", "x"))
    blocks = sum_over_chips(half_gram(core[None], mine, others, other_values, slices))
    merged, values = finish(core[None], blocks, other_values, sing_values, bases, others, points)
    return (merged[None], values)


def solution(mesh):
    fine = Mesh(mesh.devices.reshape(-1, 2, 8, 2, 4), ("y", "core", "z_hi", "z_lo", "x"))
    specs = (P(("y", "core"), ("z_hi", "z_lo", "x"), None), P(("y", "core"), None))
    return jax.shard_map(local, mesh=fine, in_specs=specs, out_specs=specs, check_vma=False)
```

```python
import functools
import math

import jax
import jax.numpy as jnp
from jax import lax
from jax.experimental import pallas as pl
from jax.experimental.pallas import tpu as pltpu
from jax.sharding import Mesh, PartitionSpec as P

ITERS = 3
NS_STEPS = 6
CHUNK = 512
FIRST = 10
FAR_FIRST = 5
GATHER_FIRST = 14
ROWS = (((0,), (0,)), ((), ()))
PLAIN = (((1,), (0,)), ((), ()))
COLUMNS = (((1,), (1,)), ((), ()))
bf16 = jnp.bfloat16
f32 = jnp.float32


def dot(a, b, dims=PLAIN):
    return lax.dot_general(a, b, dims, preferred_element_type=f32)


def split(x):
    high = x.astype(bf16)
    return high, (x - high.astype(f32)).astype(bf16)


def wide_dot(a, b, dims=PLAIN):
    (a_high, a_low), (b_high, b_low) = split(a), split(b)
    left = jnp.concatenate([a_high, a_low, a_high], axis=1)
    right = jnp.concatenate([b_high, b_high, b_low], axis=0 if dims is PLAIN else 1)
    return dot(left, right, dims)


def polar_iterate(gram):
    w = gram.shape[0] // 2
    diag = lax.broadcasted_iota(jnp.int32, (w, w), 0) == lax.broadcasted_iota(jnp.int32, (w, w), 1)
    yt = (gram[:w] + gram[w:]) * f32(1.0 / math.sqrt(2.0))
    for outer in range(ITERS):
        scale = 1.0 / (jnp.sum(yt * yt) + 1e-06)
        m = wide_dot(yt, yt, COLUMNS) * scale
        yt = yt * jnp.sqrt(scale)
        last = outer == ITERS - 1
        square = wide_dot(m, m)
        q = 1.5 * diag.astype(f32) - 0.5 * m
        for inner in range(1, NS_STEPS):
            m = 2.25 * m - 1.5 * square + 0.25 * wide_dot(square, m)
            if inner == NS_STEPS // 2:
                ahead = yt.T if last else wide_dot(yt, gram)
            if inner < NS_STEPS - 1:
                both = wide_dot(jnp.concatenate([m, q], axis=0), m)
                square = both[:w]
                q = 1.5 * q - 0.5 * both[w:]
        u = wide_dot(ahead, q) if last else wide_dot(q, ahead)
        yt = 1.5 * u - 0.5 * (wide_dot(u, m) if last else wide_dot(m, u))
    return yt


def column_squares(gram, rotation):
    high, rest = split(gram)
    low = (gram - high.astype(f32) - rest.astype(f32)).astype(bf16)
    turned = dot(high, rotation) + (dot(rest, rotation) + dot(low, rotation))
    return jnp.sum(turned * rotation.astype(f32), axis=0, keepdims=True)


def weighted(rows, weights_ref):
    return (rows.astype(f32) * weights_ref[...]).astype(bf16)


def finish_kernel(
    points, core_ref, gram_ref, other_weights_ref, weights_hbm, bases_ref, others_ref,
    out_ref, values_ref, gram_rows_ref, weights_ref, own_ref, other_ref, rows_ref, sem, out_sem,
):
    core = core_ref[0]
    rows, w = own_ref.shape
    loads = [
        pltpu.make_async_copy(bases_ref, own_ref, sem.at[0]),
        pltpu.make_async_copy(others_ref, other_ref, sem.at[1]),
        pltpu.make_async_copy(weights_hbm, weights_ref, sem.at[2]),
    ]
    for load in loads:
        load.start()
    slices, lines = gram_ref.shape[:2]
    each = w // slices
    for k in range(slices):
        for p in range(lines - 1):
            first = k * each + p if p < each else w + k * each + p - each
            gram_rows_ref[first : first + 1] = gram_ref[(k - GATHER_FIRST) % slices, p]
    shared, ab = gram_rows_ref[:w], gram_rows_ref[w:]
    turned = shared.T
    row = lax.broadcasted_iota(jnp.int32, (w, w), 0)
    column = lax.broadcasted_iota(jnp.int32, (w, w), 1)
    aa = jnp.where(row <= column, shared, turned)
    bb = jnp.where(row > column, shared, jnp.where(row < column, turned, gram_ref[0, lines - 1]))
    gram = jnp.concatenate(
        [jnp.concatenate([aa, ab], axis=1), jnp.concatenate([ab.T, bb], axis=1)], axis=0
    )
    rotation = polar_iterate(gram).astype(bf16)
    for load in loads:
        load.wait()
    squares = column_squares(gram, rotation)
    values = jnp.sqrt(jnp.maximum(squares, 0.0) / points + 1e-06)
    values_ref[...] = values
    inverse = 1.0 / values
    swapped = jnp.concatenate([rotation[w:], rotation[:w]], axis=0)
    rotation = jnp.where(core == 0, rotation, swapped)
    copies = []
    for j in range(rows // CHUNK):
        part = pl.ds(j * CHUNK, CHUNK)
        own = weighted(own_ref[part], weights_ref)
        stacked = jnp.concatenate([own, weighted(other_ref[part], other_weights_ref)], axis=1)
        rows_ref[part] = (dot(stacked, rotation) * inverse).astype(bf16)
        copies.append(pltpu.make_async_copy(rows_ref.at[part], out_ref.at[part], out_sem.at[j]))
        copies[-1].start()
    for copy in copies:
        copy.wait()


def finish(core, blocks, other_values, sing_values, bases, others, points):
    rows, w = bases.shape
    smem, vmem, hbm, anywhere = (
        pl.BlockSpec(memory_space=space) for space in (pltpu.SMEM, pltpu.VMEM, pltpu.HBM, pl.ANY)
    )
    return pl.pallas_call(
        functools.partial(finish_kernel, points),
        in_specs=[smem, vmem, vmem, hbm, hbm, anywhere],
        out_specs=[anywhere, vmem],
        out_shape=[jax.ShapeDtypeStruct((rows, w), bf16), jax.ShapeDtypeStruct((1, w), f32)],
        scratch_shapes=[
            pltpu.VMEM((2 * w, w), f32),
            pltpu.VMEM(sing_values.shape, f32),
            pltpu.VMEM((rows, w), bf16),
            pltpu.VMEM((rows, w), bf16),
            pltpu.VMEM((rows, w), bf16),
            pltpu.SemaphoreType.DMA((3,)),
            pltpu.SemaphoreType.DMA((rows // CHUNK,)),
        ],
        compiler_params=pltpu.CompilerParams(vmem_limit_bytes=16 << 20),
    )(core, blocks, other_values, sing_values, bases, others)


def weigh_kernel(core_ref, weights_hbm, bases_ref, out_ref, weights_ref, rows_ref, sem):
    half = out_ref.shape[0]
    steps = half // CHUNK
    weights = pltpu.make_async_copy(weights_hbm, weights_ref, sem.at[steps])
    weights.start()
    copies = []
    for j in range(steps):
        first = pl.multiple_of((core_ref[0] * steps + j) * CHUNK, CHUNK)
        here = rows_ref.at[pl.ds(j * CHUNK, CHUNK)]
        copies.append(pltpu.make_async_copy(bases_ref.at[pl.ds(first, CHUNK)], here, sem.at[j]))
        copies[-1].start()
    weights.wait()
    for j, copy in enumerate(copies):
        copy.wait()
        part = pl.ds(j * CHUNK, CHUNK)
        out_ref[part] = weighted(rows_ref[part], weights_ref)


def weigh(core, sing_values, bases):
    rows, w = bases.shape
    vmem, hbm = (pl.BlockSpec(memory_space=space) for space in (pltpu.VMEM, pltpu.HBM))
    return pl.pallas_call(
        weigh_kernel,
        in_specs=[pl.BlockSpec(memory_space=pltpu.SMEM), hbm, hbm],
        out_specs=vmem,
        out_shape=pltpu.VMEM((rows // 2, w), bf16),
        scratch_shapes=[
            pltpu.VMEM(sing_values.shape, f32),
            pltpu.VMEM((rows // 2, w), bf16),
            pltpu.SemaphoreType.DMA((rows // 2 // CHUNK + 1,)),
        ],
        compiler_params=pltpu.CompilerParams(vmem_limit_bytes=8 << 20),
    )(core, sing_values, bases)


def gram_kernel(core_ref, own_ref, others_ref, other_weights_ref, out_ref):
    half, w = own_ref.shape
    first = pl.multiple_of(core_ref[0] * half, half)
    other = weighted(others_ref[pl.ds(first, half)], other_weights_ref)
    stacked = jnp.concatenate([own_ref[...], other], axis=1)
    gram = dot(stacked, stacked, ROWS)
    even = core_ref[0] == 0
    own, other = gram[:w, :w], gram[w:, w:]
    across = jnp.where(even, gram[:w, w:], gram[w:, :w])
    aa, bb = jnp.where(even, own, other), jnp.where(even, other, own)
    row = lax.broadcasted_iota(jnp.int32, (w, w), 0)
    column = lax.broadcasted_iota(jnp.int32, (w, w), 1)
    shared = jnp.where(row <= column, aa, bb)
    diag = jnp.sum(jnp.where(row == column, bb, 0.0), axis=0, keepdims=True)
    slices, lines = out_ref.shape[:2]
    each = w // slices
    for k in range(slices):
        for p in range(each):
            first = k * each + p
            out_ref[(k - FIRST) % slices, p] = shared[first : first + 1]
            out_ref[(k - FIRST) % slices, each + p] = across[first : first + 1]
        out_ref[k, lines - 1] = diag


def half_gram(core, own, others, other_values, slices):
    w = own.shape[1]
    vmem = pl.BlockSpec(memory_space=pltpu.VMEM)
    return pl.pallas_call(
        gram_kernel,
        in_specs=[pl.BlockSpec(memory_space=pltpu.SMEM)] + [vmem] * 3,
        out_specs=vmem,
        out_shape=jax.ShapeDtypeStruct((slices, 2 * (w // slices) + 1, 1, w), f32),
        compiler_params=pltpu.CompilerParams(vmem_limit_bytes=12 << 20),
    )(core, own, others, other_values)


def sum_over_chips(part):
    near, far = ("core", "z_lo", "x"), "z_hi"
    n, m = part.shape[0], lax.axis_size(far)

    def turned(size, first):
        return [[(i + first) % size for i in range(size)]]

    part = lax.all_to_all(part, near, 0, 0, axis_index_groups=turned(n, FIRST))
    part = jnp.broadcast_to(jnp.sum(part, axis=0)[None], (m, *part.shape[1:]))
    part = lax.all_to_all(part, far, 0, 0, axis_index_groups=turned(m, FAR_FIRST))
    part = jnp.broadcast_to(jnp.sum(part, axis=0)[None], (n, *part.shape[1:]))
    return lax.all_to_all(part, near, 0, 0, axis_index_groups=turned(n, GATHER_FIRST))


def local(bases, sing_values):
    rows = bases.shape[1]
    points = rows * math.prod(lax.axis_size(axis) for axis in ("z_hi", "z_lo", "x"))
    core = lax.axis_index("core").astype(jnp.int32)

    def partners(value):
        return lax.ppermute(value, "core", [(0, 1), (1, 0)])

    others, other_values = partners(bases[0]), partners(sing_values)
    bases = pltpu.with_memory_space_constraint(bases[0], pltpu.HBM)
    sing_values = pltpu.with_memory_space_constraint(sing_values, pltpu.HBM)
    mine = weigh(core[None], sing_values, bases)
    slices = math.prod(lax.axis_size(axis) for axis in ("core", "z_lo", "x"))
    blocks = sum_over_chips(half_gram(core[None], mine, others, other_values, slices))
    merged, values = finish(core[None], blocks, other_values, sing_values, bases, others, points)
    return (merged[None], values)


def solution(mesh):
    fine = Mesh(mesh.devices.reshape(-1, 2, 8, 2, 4), ("y", "core", "z_hi", "z_lo", "x"))
    specs = (P(("y", "core"), ("z_hi", "z_lo", "x"), None), P(("y", "core"), None))
    return jax.shard_map(local, mesh=fine, in_specs=specs, out_specs=specs, check_vma=False)
```
